512 devices in a mesh: batch: 16 (over y, z_hi), space: 32 (over x, z_lo, core).
Axes of the slice: x: 4, y: 4, z: 16 (z_hi: 4, z_lo: 4; z = z_hi * 4 + z_lo), core: 2. Of those that a mesh axis runs over, the one named last changes fastest.
Arguments:
- latent: bfloat16 [65536, 640], P(('batch', 'space')), parts along dimension 0, may hold values from -8 to 8
- timestep: int32 [16], P('batch'), parts along dimension 0, may hold values from 0 to 999
- norm1_gain: float32 [640], replicated, may hold values from 0.25 to 1.75
- norm1_shift: float32 [640], replicated, may hold values from -3 to 3
- conv_weight: bfloat16 [5760, 640], P('space'), may hold values from -0.078125 to 0.078125
- conv_bias: float32 [640], replicated, may hold values from -3 to 3
- time_weight: float32 [320, 640], replicated, may hold values from -0.5 to 0.5
- norm2_gain: float32 [640], replicated, may hold values from 0.25 to 1.75
- norm2_shift: float32 [640], replicated, may hold values from -3 to 3
- qkv_weight: bfloat16 [640, 960], replicated, may hold values from -0.25 to 0.25
- out_weight: bfloat16 [320, 640], replicated, may hold values from -0.3125 to 0.3125
- stale_kv: bfloat16 [2, 65536, 320], P(None, ('batch', 'space')), parts along dimension 1, may hold values from -6 to 6
Outputs:
- result: bfloat16 [65536, 640], P(('batch', 'space')), parts along dimension 0
- fresh_kv: bfloat16 [2, 65536, 320], P(None, ('batch', 'space')), parts along dimension 1
The draws below stay inside these ranges and needn't reach their ends.
There are 16 independent parts, one for each index of `batch`. The reference program is written for one: setup_inputs(seed, part) draws one part's arguments, and reference() takes and returns one part's arrays. A program takes and returns all parts, laid end to end along the dimension named above; an argument that names none is the same for every part. Nothing has to cross between parts.
All inputs are finite; a program needn't handle non-finite values.
Results may differ from the reference program's by a relative error of at most 0.015.
Values may be sent and summed in bfloat16 or wider, within the bound.
No kernel may reach another device: no remote copies, remote signals or barrier semaphores. Data moves between devices by JAX's collectives and lax.ppermute only.
A program may use at most 64 MiB of HBM per device.

```python
import math
import jax
import jax.numpy as jnp
from jax import lax

C = 640
GROUPS = 32
HEADS = 5
HEAD_DIM = 64
TFREQ = 320
GW = 128
HD = 320
TOK_DEV = 128
GH = 32
TOKENS = 4096
N_SPACE = 32


def draw_latent(key, part):
    key = jax.random.fold_in(key, 11)
    noise_key, chan_key = jax.random.split(key)
    row = (jnp.arange(TOKENS, dtype=jnp.int32) // GW).astype(jnp.float32)
    ramp = (row / max(GH - 1, 1))[:, None]
    chan = jax.random.uniform(chan_key, (1, C), jnp.float32, 0.6, 1.4)
    noise = jax.random.normal(noise_key, (TOKENS, C), jnp.float32)
    offset = (0.5 + ramp) * chan
    spread = 0.8 + 0.4 * ramp
    return jnp.clip(offset + spread * noise, -8.0, 8.0).astype(jnp.bfloat16)


def level_of(own_key, shape, shards, least, largest):
    def one(dim, shards_of):
        heights = jax.random.uniform(jax.random.fold_in(jax.random.fold_in(own_key, 6), dim), (shards_of,), jnp.float32, least / len(shards), largest / len(shards))
        return jnp.repeat(jnp.exp(heights), shape[dim] // shards_of).reshape((-1,) + (1,) * (len(shape) - dim - 1))

    level = one(*shards[0])
    for cut in shards[1:]:
        level = level * one(*cut)
    return level


def bell_draw(stream_key, shape, scale, reach, cuts=(), held_as=jnp.bfloat16):
    values = scale * jax.random.normal(stream_key, shape, jnp.float32)
    if cuts:
        values = values * level_of(stream_key, shape, cuts, -0.22, 0.18)
    return jnp.clip(values, -reach, reach).astype(held_as)


def setup_inputs(seed: int = 0, part: int = 0) -> dict:
    splits = jax.random.split(jax.random.key(seed), 13)
    part_splits = jax.random.split(jax.random.fold_in(splits[12], part), 13)
    return {
        "latent": draw_latent(jax.random.fold_in(jax.random.fold_in(splits[12], part), 71), part),
        "timestep": jax.random.randint(part_splits[1], (1,), 0, 1000).astype(jnp.int32),
        "norm1_gain": jnp.clip(1.0 + 0.15 * jax.random.normal(splits[2], (C,), jnp.float32), 0.25, 1.75),
        "norm1_shift": bell_draw(splits[3], (C,), 0.5, 3.0, (), jnp.float32),
        "conv_weight": bell_draw(splits[4], (9 * C, C), (9 * C) ** -0.5, 0.078125, ((0, 32),)),
        "conv_bias": bell_draw(splits[5], (C,), 0.5, 3.0, (), jnp.float32),
        "time_weight": bell_draw(splits[6], (TFREQ, C), (TFREQ // 2) ** -0.5, 0.5, (), jnp.float32),
        "norm2_gain": jnp.clip(1.0 + 0.15 * jax.random.normal(splits[7], (C,), jnp.float32), 0.25, 1.75),
        "norm2_shift": bell_draw(splits[8], (C,), 0.5, 3.0, (), jnp.float32),
        "qkv_weight": bell_draw(splits[9], (C, 3 * HD), C ** -0.5, 0.25),
        "out_weight": bell_draw(splits[10], (HD, C), HD ** -0.5, 0.3125),
        "stale_kv": bell_draw(part_splits[11], (2, TOKENS, HD), 1.0, 6.0, ((1, 32),)),
    }


def group_norm(values, gain, shift, eps):
    count, width = values.shape
    grouped = values.reshape(count, GROUPS, width // GROUPS)
    mean = lax.optimization_barrier(jnp.mean(grouped, axis=(0, 2)))
    centered = grouped - mean[None, :, None]
    var = lax.optimization_barrier(jnp.mean(centered * centered, axis=(0, 2)))
    scaled = centered * lax.rsqrt(var + eps)[None, :, None]
    return scaled.reshape(count, width) * gain + shift

def time_embed(timestep, time_weight):
    half = TFREQ // 2
    index = jnp.arange(half, dtype=jnp.float32)
    freq = jnp.exp(-math.log(10000.0) * index / half)
    angle = timestep.astype(jnp.float32)[0] * freq
    feats = jnp.concatenate([jnp.cos(angle), jnp.sin(angle)])[None, :]
    return jnp.dot(feats, time_weight, precision=lax.Precision.HIGHEST)

def reference(latent, timestep, norm1_gain, norm1_shift, conv_weight, conv_bias, time_weight, norm2_gain, norm2_shift, qkv_weight, out_weight, stale_kv):
    base = latent.astype(jnp.float32)
    normed = jax.nn.silu(group_norm(base, norm1_gain, norm1_shift, 1e-05)).astype(jnp.bfloat16)
    padded = jnp.pad(normed.reshape(GH, GW, C), ((1, 1), (1, 1), (0, 0)))
    conv = jnp.zeros((TOKENS, C), jnp.float32)
    for tap in range(9):
        down, across = (tap // 3, tap % 3)
        window = padded[down:down + GH, across:across + GW].reshape(TOKENS, C)
        conv = conv + jnp.dot(window, conv_weight[tap * C:(tap + 1) * C], preferred_element_type=jnp.float32)
    mid = (base + conv + conv_bias + time_embed(timestep, time_weight)).astype(jnp.bfloat16)
    normed2 = group_norm(mid.astype(jnp.float32), norm2_gain, norm2_shift, 1e-06).astype(jnp.bfloat16)
    qkv = jnp.dot(normed2, qkv_weight, preferred_element_type=jnp.float32).astype(jnp.bfloat16)
    query, key, value = (qkv[:, :HD], qkv[:, HD:2 * HD], qkv[:, 2 * HD:])
    fresh_kv = jnp.stack([key, value])
    scale = 1.0 / math.sqrt(HEAD_DIM)

    def patch(index):
        start = (index * TOK_DEV).astype(jnp.int32)
        queries = lax.dynamic_slice_in_dim(query, start, TOK_DEV, 0).reshape(TOK_DEV, HEADS, HEAD_DIM)
        keys = lax.dynamic_update_slice_in_dim(stale_kv[0], lax.dynamic_slice_in_dim(key, start, TOK_DEV, 0), start, 0)
        values = lax.dynamic_update_slice_in_dim(stale_kv[1], lax.dynamic_slice_in_dim(value, start, TOK_DEV, 0), start, 0)
        keys = keys.reshape(TOKENS, HEADS, HEAD_DIM).astype(jnp.float32)
        values = values.reshape(TOKENS, HEADS, HEAD_DIM).astype(jnp.float32)
        scores = jnp.einsum('qhd,khd->hqk', queries.astype(jnp.float32), keys) * scale
        peak = lax.optimization_barrier(jnp.max(scores, axis=-1, keepdims=True))
        expo = jnp.exp(scores - peak)
        total = lax.optimization_barrier(jnp.sum(expo, axis=-1))
        weights = expo.astype(jnp.bfloat16).astype(jnp.float32)
        mixed = jnp.einsum('hqk,khd->hqd', weights, values) / total[:, :, None]
        return mixed.transpose(1, 0, 2).reshape(TOK_DEV, HD)
    attended = lax.map(patch, jnp.arange(N_SPACE, dtype=jnp.int32)).reshape(TOKENS, HD).astype(jnp.bfloat16)
    result = (mid.astype(jnp.float32) + jnp.dot(attended, out_weight, preferred_element_type=jnp.float32)).astype(jnp.bfloat16)
    return (result, fresh_kv)
```

```python
import math

import jax
import jax.numpy as jnp
from jax import lax
from jax.sharding import PartitionSpec as P

GROUPS = 32
HEADS = 5
HEAD_DIM = 64
TFREQ = 320
GW = 128


def local_stats(values):
    count, width = values.shape
    per = width // GROUPS
    mean = jnp.sum(values, axis=0).reshape(GROUPS, per).sum(axis=1) / (count * per)
    centered = values - jnp.repeat(mean, per)
    spread = jnp.sum(centered * centered, axis=0).reshape(GROUPS, per).sum(axis=1)
    return jnp.concatenate([mean, spread])


def merged_stats(values, eps):
    count, width = values.shape
    per = width // GROUPS
    peers = lax.axis_size("space")
    mine = local_stats(values)
    every = lax.all_to_all(
        jnp.broadcast_to(mine[None, None], (peers, 1, 2 * GROUPS)), "space", 0, 0, tiled=True
    )[:, 0]
    means, spreads = every[:, :GROUPS], every[:, GROUPS:]
    mean = jnp.mean(means, axis=0)
    shifted = means - mean
    var = (
        jnp.sum(spreads, axis=0) / (count * per) + jnp.sum(shifted * shifted, axis=0)
    ) / peers
    return jnp.repeat(mean, per), jnp.repeat(lax.rsqrt(var + eps), per)


def time_embed(timestep, time_weight):
    half = TFREQ // 2
    index = jnp.arange(half, dtype=jnp.float32)
    freq = jnp.exp(-math.log(10000.0) * index / half)
    angle = timestep.astype(jnp.float32)[0] * freq
    feats = jnp.concatenate([jnp.cos(angle), jnp.sin(angle)])[None, :]
    return jnp.dot(feats, time_weight, precision=lax.Precision.HIGHEST)


def on_device(
    latent,
    timestep,
    norm1_gain,
    norm1_shift,
    conv_weight,
    conv_bias,
    time_weight,
    norm2_gain,
    norm2_shift,
    qkv_weight,
    out_weight,
    stale_kv,
):
    tok_dev, width = latent.shape
    peers = lax.axis_size("space")
    me = lax.axis_index("space")
    rows = conv_weight.shape[0]
    sent = jnp.concatenate(
        [conv_weight, jnp.concatenate([stale_kv[0], stale_kv[1]], axis=1)], axis=0
    )
    whole = lax.all_gather(sent, "space", axis=0)
    up = [(i, i + 1) for i in range(peers - 1)]
    down = [(i + 1, i) for i in range(peers - 1)]
    before = lax.ppermute(latent, "space", up)
    after = lax.ppermute(latent, "space", down)
    base = latent.astype(jnp.float32)
    mean, scale1 = merged_stats(base, 1e-05)
    three = jnp.stack([before, latent, after]).astype(jnp.float32)
    normed = jax.nn.silu((three - mean) * scale1 * norm1_gain + norm1_shift).astype(jnp.bfloat16)
    inside = jnp.stack([me > 0, me >= 0, me < peers - 1])
    normed = jnp.where(inside[:, None, None], normed, 0)
    padded = jnp.pad(normed, ((0, 0), (1, 1), (0, 0)))
    windows = []
    for tap in range(9):
        down_, across = (tap // 3, tap % 3)
        windows.append(padded[down_, across : across + GW])
    unfolded = jnp.concatenate(windows, axis=1)
    bias = conv_bias + time_embed(timestep, time_weight)
    weight = whole[:, :rows].reshape(peers * rows, width)
    conv = jnp.dot(unfolded, weight, preferred_element_type=jnp.float32)
    mid = (base + conv + bias).astype(jnp.bfloat16)
    mid32 = mid.astype(jnp.float32)
    mean2, scale2 = merged_stats(mid32, 1e-06)
    normed2 = ((mid32 - mean2) * scale2 * norm2_gain + norm2_shift).astype(jnp.bfloat16)
    qkv = jnp.dot(normed2, qkv_weight, preferred_element_type=jnp.float32).astype(jnp.bfloat16)
    feats = qkv.shape[1] // 3
    query, key, value = (qkv[:, :feats], qkv[:, feats : 2 * feats], qkv[:, 2 * feats :])
    fresh_kv = jnp.stack([key, value])
    held = whole[:, rows:]
    own = (jnp.arange(peers) == me)[:, None, None]
    held = jnp.where(own, qkv[:, feats:], held).reshape(peers * tok_dev, 2 * feats)
    keys = held[:, :feats].reshape(-1, HEADS, HEAD_DIM)
    values = held[:, feats:].reshape(-1, HEADS, HEAD_DIM)
    queries = query.reshape(tok_dev, HEADS, HEAD_DIM)
    scores = jnp.einsum(
        "qhd,khd->hqk", queries, keys, preferred_element_type=jnp.float32
    ) * (1.0 / math.sqrt(HEAD_DIM))
    peak = jnp.max(scores, axis=-1, keepdims=True)
    expo = jnp.exp(scores - peak)
    total = jnp.sum(expo, axis=-1)
    mixed = jnp.einsum(
        "hqk,khd->hqd", expo.astype(jnp.bfloat16), values, preferred_element_type=jnp.float32
    )
    attended = (
        (mixed / total[:, :, None]).transpose(1, 0, 2).reshape(tok_dev, feats).astype(jnp.bfloat16)
    )
    result = (
        mid32 + jnp.dot(attended, out_weight, preferred_element_type=jnp.float32)
    ).astype(jnp.bfloat16)
    return (result, fresh_kv)


def solution(mesh):
    return jax.shard_map(
        on_device,
        mesh=mesh,
        in_specs=(
            P(("batch", "space"), None),
            P("batch"),
            P(),
            P(),
            P("space", None),
            P(),
            P(),
            P(),
            P(),
            P(),
            P(),
            P(None, ("batch", "space"), None),
        ),
        out_specs=(P(("batch", "space"), None), P(None, ("batch", "space"), None)),
        check_vma=False,
    )
```

```python
import math

import jax
import jax.numpy as jnp
from jax import lax
from jax.experimental import pallas as pl
from jax.experimental.pallas import tpu as pltpu
from jax.sharding import PartitionSpec as P

GROUPS = 32
HEADS = 5
HEAD_DIM = 64
TFREQ = 320
GW = 128
PEERS = 32
Z_GROUPS = [[8 * x + 2 * z + c for z in range(4)] for x in range(4) for c in range(2)]
CORE_GROUPS = [[2 * k, 2 * k + 1] for k in range(16)]
RIGHT = [(i, (i + 8) % PEERS) for i in range(PEERS)]
LEFT = [(i, (i + 24) % PEERS) for i in range(PEERS)]
SWAP = [(i, i ^ 1) for i in range(PEERS)]
OUTER = [(i, i - 2) for i in range(2, PEERS, 2)] + [(i, i + 2) for i in range(1, PEERS - 2, 2)]
ROWS = 192
LOW = -1e30
VMEM = pl.BlockSpec(memory_space=pltpu.VMEM)
SMEM = pl.BlockSpec(memory_space=pltpu.SMEM)


def local_stats(values):
    count, width = values.shape
    per = width // GROUPS
    mean = jnp.sum(values, axis=0).reshape(GROUPS, per).sum(axis=1) / (count * per)
    centered = values - jnp.repeat(mean, per)
    spread = jnp.sum(centered * centered, axis=0).reshape(GROUPS, per).sum(axis=1)
    return jnp.concatenate([mean, spread])


def merged_stats(values, eps):
    count, width = values.shape
    per = width // GROUPS
    mine = local_stats(values)
    every = lax.all_to_all(
        jnp.broadcast_to(mine[None, None], (PEERS, 1, 2 * GROUPS)), "space", 0, 0, tiled=True
    )[:, 0]
    means, spreads = every[:, :GROUPS], every[:, GROUPS:]
    mean = jnp.mean(means, axis=0)
    shifted = means - mean
    var = (
        jnp.sum(spreads, axis=0) / (count * per) + jnp.sum(shifted * shifted, axis=0)
    ) / PEERS
    return jnp.repeat(mean, per), jnp.repeat(lax.rsqrt(var + eps), per)


def time_embed(timestep, time_weight):
    half = TFREQ // 2
    index = jnp.arange(half, dtype=jnp.float32)
    freq = jnp.exp(-math.log(10000.0) * index / half)
    angle = timestep.astype(jnp.float32)[0] * freq
    feats = jnp.concatenate([jnp.cos(angle), jnp.sin(angle)])[None, :]
    return jnp.dot(feats, time_weight, precision=lax.Precision.HIGHEST)


def dot32(a, b):
    return jnp.dot(a, b, preferred_element_type=jnp.float32)


def conv_near(x_ref, blocks_ref, own_ref, left_ref, right_ref, out_ref):
    x = x_ref[0]
    total = None
    for step, ref in ((0, own_ref), (3, left_ref), (1, right_ref)):
        first = 4 * ((x + step) & 3)
        for z in range(4):
            part = dot32(blocks_ref[first + z], ref[z])
            total = part if total is None else total + part
    out_ref[...] = total


def conv_far(x_ref, blocks_ref, low_ref, high_ref, near_ref, out_ref):
    first = 4 * ((x_ref[0] + 2) & 3)
    total = near_ref[...]
    for z in range(4):
        ref = low_ref if z < 2 else high_ref
        total = total + dot32(blocks_ref[first + z], ref[z % 2])
    out_ref[...] = total


def attend(z_ref, q_ref, own_ref, left_ref, right_ref, low_ref, high_ref, fresh_ref, out_ref):
    my_z = z_ref[0]
    count = fresh_ref.shape[0]
    lane = lax.broadcasted_iota(jnp.int32, (2 * count, 128), 1)
    row = lax.broadcasted_iota(jnp.int32, (2 * count, 4 * count), 0)
    block = lax.broadcasted_iota(jnp.int32, (2 * count, 4 * count), 1) // count
    replaced = (row < count) & (block == my_z)
    held = (own_ref, left_ref, right_ref, low_ref, high_ref)
    outs = []
    for head in range(HEADS):
        k_at = 128 * ((HEADS + head) // 2)
        v_at = 128 * (head // 2)
        q_at = 128 * ((1 + head) // 2)
        mine = (lane >= 64) if head % 2 == 0 else (lane < 64)
        query = jnp.where(mine, q_ref[:, q_at : q_at + 128].astype(jnp.float32), 0.0)
        query = query.astype(jnp.bfloat16)
        scores = []
        for ref in held:
            keys = ref[:, :, k_at : k_at + 128].reshape(-1, 128)
            scores.append(
                lax.dot_general(
                    query, keys, (((1,), (1,)), ((), ())), preferred_element_type=jnp.float32
                )
            )
        scores[0] = jnp.where(replaced, LOW, scores[0])
        fresh = lax.dot_general(
            query[:count],
            fresh_ref[:, k_at : k_at + 128],
            (((1,), (1,)), ((), ())),
            preferred_element_type=jnp.float32,
        )
        scores.append(jnp.concatenate([fresh, jnp.full((count, count), LOW, jnp.float32)], axis=0))
        peak = scores[0].max(axis=1, keepdims=True)
        for s in scores[1:]:
            peak = jnp.maximum(peak, s.max(axis=1, keepdims=True))
        total = jnp.zeros((2 * count, 1), jnp.float32)
        mixed = jnp.zeros((2 * count, 128), jnp.float32)
        for s, ref in zip(scores, held + (fresh_ref,), strict=True):
            weights = jnp.exp(s - peak)
            total = total + weights.sum(axis=1, keepdims=True)
            if ref is fresh_ref:
                values = ref[:, v_at : v_at + 128]
            else:
                values = ref[:, :, v_at : v_at + 128].reshape(-1, 128)
            mixed = mixed + dot32(weights.astype(jnp.bfloat16), values)
        outs.append((mixed, peak, total))
    out_ref[:, :128] = jnp.where(lane < 64, outs[0][0], outs[1][0])
    out_ref[:, 128:256] = jnp.where(lane < 64, outs[2][0], outs[3][0])
    last = jnp.where(lane < 64, outs[4][0], 0.0)
    for head in range(HEADS):
        last = jnp.where(lane == 64 + head, outs[head][1], last)
        last = jnp.where(lane == 72 + head, outs[head][2], last)
    out_ref[:, 256:] = last


def finish(own_ref, other_ref, mid_ref, weight_ref, out_ref):
    count = mid_ref.shape[0]
    lane = lax.broadcasted_iota(jnp.int32, (count, 128), 1)
    factors = []
    for head in range(HEADS):
        peak1 = own_ref[:, 320 + head : 321 + head]
        peak2 = other_ref[:, 320 + head : 321 + head]
        peak = jnp.maximum(peak1, peak2)
        one, two = jnp.exp(peak1 - peak), jnp.exp(peak2 - peak)
        total = own_ref[:, 328 + head : 329 + head] * one
        total = total + other_ref[:, 328 + head : 329 + head] * two
        factors.append((one / total, two / total))
    result = mid_ref[...].astype(jnp.float32)
    for tile in range(3):
        first = factors[2 * tile]
        second = factors[min(2 * tile + 1, HEADS - 1)]
        at = 128 * tile
        mixed = own_ref[:, at : at + 128] * jnp.where(lane < 64, first[0], second[0])
        mixed = mixed + other_ref[:, at : at + 128] * jnp.where(lane < 64, first[1], second[1])
        if tile == 2:
            mixed = jnp.where(lane < 64, mixed, 0.0)
        result = result + dot32(mixed.astype(jnp.bfloat16), weight_ref[at : at + 128])
    out_ref[...] = result.astype(jnp.bfloat16)


def call(kernel, shape, dtype, specs, *args):
    return pl.pallas_call(
        kernel,
        out_shape=jax.ShapeDtypeStruct(shape, dtype),
        in_specs=specs,
        out_specs=VMEM,
        compiler_params=pltpu.CompilerParams(vmem_limit_bytes=40 * 1024 * 1024),
    )(*args)


def on_device(
    latent,
    timestep,
    norm1_gain,
    norm1_shift,
    conv_weight,
    conv_bias,
    time_weight,
    norm2_gain,
    norm2_shift,
    qkv_weight,
    out_weight,
    stale_kv,
):
    tok_dev, width = latent.shape
    me = lax.axis_index("space")
    x, z, core = me // 8, (me // 2) % 4, me % 2
    x_at, z_at = x.reshape(1), z.reshape(1)
    rows = conv_weight.shape[0]

    outer = lax.ppermute(latent, "space", OUTER)
    base = latent.astype(jnp.float32)
    mean, scale1 = merged_stats(base, 1e-05)

    weight = jnp.pad(conv_weight, ((0, ROWS - rows), (0, 0)))
    own_w = lax.all_gather(weight, "space", axis=0, axis_index_groups=Z_GROUPS)
    left_w = lax.ppermute(own_w, "space", RIGHT)
    right_w = lax.ppermute(own_w, "space", LEFT)
    low_w = lax.ppermute(left_w[:2], "space", RIGHT)
    high_w = lax.ppermute(right_w[2:], "space", LEFT)

    stale = jnp.concatenate([stale_kv[1], stale_kv[0]], axis=1)
    stale, _ = lax.optimization_barrier((stale, own_w))
    own_kv = lax.all_gather(stale, "space", axis=0, axis_index_groups=Z_GROUPS)

    pair = lax.all_gather(
        jnp.stack([latent, outer]), "space", axis=0, axis_index_groups=CORE_GROUPS
    )
    four = jnp.stack([pair[1, 1], pair[0, 0], pair[1, 0], pair[0, 1]]).astype(jnp.float32)
    normed = jax.nn.silu((four - mean) * scale1 * norm1_gain + norm1_shift).astype(jnp.bfloat16)
    inside = jnp.stack([me >= 2, me >= 0, me >= 0, me < PEERS - 2])
    normed = jnp.where(inside[:, None, None], normed, 0)
    padded = jnp.pad(normed, ((0, 0), (1, 1), (0, 0)))
    unfolded = jnp.concatenate(
        [padded[t // 3 : t // 3 + 2, t % 3 : t % 3 + GW] for t in range(9)], axis=2
    )
    blocks = unfolded.reshape(2 * tok_dev, 16, 2, rows)
    blocks = lax.dynamic_index_in_dim(blocks, core, axis=2, keepdims=False).transpose(1, 0, 2)
    blocks = jnp.pad(blocks, ((0, 0), (0, 0), (0, ROWS - rows)))

    shape = (2 * tok_dev, width)
    near = call(
        conv_near, shape, jnp.float32, [SMEM] + [VMEM] * 4, x_at, blocks, own_w, left_w, right_w
    )
    sums = call(
        conv_far, shape, jnp.float32, [SMEM] + [VMEM] * 4, x_at, blocks, low_w, high_w, near
    )
    sums = sums.reshape(2, tok_dev, width)
    kept = lax.dynamic_index_in_dim(sums, core, axis=0, keepdims=False)
    given = lax.dynamic_index_in_dim(sums, 1 - core, axis=0, keepdims=False)
    conv = kept + lax.ppermute(given, "space", SWAP)

    own_kv, _ = lax.optimization_barrier((own_kv, sums))
    left_kv = lax.ppermute(own_kv, "space", RIGHT)
    right_kv = lax.ppermute(own_kv, "space", LEFT)
    low_kv = lax.ppermute(left_kv[:2], "space", RIGHT)
    high_kv = lax.ppermute(right_kv[2:], "space", LEFT)

    bias = conv_bias + time_embed(timestep, time_weight)
    mid = (base + conv + bias).astype(jnp.bfloat16)
    mid32 = mid.astype(jnp.float32)
    mean2, scale2 = merged_stats(mid32, 1e-06)
    normed2 = ((mid32 - mean2) * scale2 * norm2_gain + norm2_shift).astype(jnp.bfloat16)
    qkv = dot32(normed2, qkv_weight).astype(jnp.bfloat16)
    feats = qkv.shape[1] // 3
    query, key, value = (qkv[:, :feats], qkv[:, feats : 2 * feats], qkv[:, 2 * feats :])
    fresh_kv = jnp.stack([key, value])
    fresh = jnp.concatenate([value, key], axis=1)
    query = jnp.pad(query * (1.0 / math.sqrt(HEAD_DIM)), ((0, 0), (HEAD_DIM, 0)))
    both = jnp.concatenate([query, lax.ppermute(query, "space", SWAP)], axis=0)
    parts = call(
        attend,
        (2 * tok_dev, 384),
        jnp.float32,
        [SMEM] + [VMEM] * 7,
        z_at,
        both,
        own_kv,
        left_kv,
        right_kv,
        low_kv,
        high_kv,
        fresh,
    )
    other = lax.ppermute(parts[tok_dev:], "space", SWAP)
    project = jnp.pad(out_weight, ((0, 384 - feats), (0, 0)))
    result = call(
        finish, (tok_dev, width), jnp.bfloat16, [VMEM] * 4, parts[:tok_dev], other, mid, project
    )
    return (result, fresh_kv)


def solution(mesh):
    return jax.shard_map(
        on_device,
        mesh=mesh,
        in_specs=(
            P(("batch", "space"), None),
            P("batch"),
            P(),
            P(),
            P("space", None),
            P(),
            P(),
            P(),
            P(),
            P(),
            P(),
            P(None, ("batch", "space"), None),
        ),
        out_specs=(P(("batch", "space"), None), P(None, ("batch", "space"), None)),
        check_vma=False,
    )
```

```python
import math

import jax
import jax.numpy as jnp
from jax import lax
from jax.experimental import pallas as pl
from jax.experimental.pallas import tpu as pltpu
from jax.sharding import PartitionSpec as P

GROUPS = 32
HEADS = 5
HEAD_DIM = 64
TFREQ = 320
PER = 20
PEERS = 32
Z_GROUPS = [[8 * x + 2 * z + c for z in range(4)] for x in range(4) for c in range(2)]
CORE_GROUPS = [[2 * k, 2 * k + 1] for k in range(16)]
RIGHT = [(i, (i + 8) % PEERS) for i in range(PEERS)]
LEFT = [(i, (i + 24) % PEERS) for i in range(PEERS)]
SWAP = [(i, i ^ 1) for i in range(PEERS)]
OUTER = [(i, i - 2) for i in range(2, PEERS, 2)] + [(i, i + 2) for i in range(1, PEERS - 2, 2)]
ROWS = 192
LOW = -1e30
VMEM = pl.BlockSpec(memory_space=pltpu.VMEM)
SMEM = pl.BlockSpec(memory_space=pltpu.SMEM)


def group_map(first, transposed=False):
    shape = (128, 640) if transposed else (640, 128)
    channel = lax.broadcasted_iota(jnp.int32, shape, 1 if transposed else 0)
    low = (lax.broadcasted_iota(jnp.int32, shape, 0 if transposed else 1) - first) * PER
    return ((channel >= low) & (channel < low + PER)).astype(jnp.float32)


def exact(a, b):
    return jnp.dot(
        a, b, precision=lax.Precision.HIGHEST, preferred_element_type=jnp.float32
    )


def local_stats(values):
    count, width = values.shape
    summed = jnp.broadcast_to(values.sum(axis=0, keepdims=True), (8, width))
    mean = exact(summed, group_map(0)) / (count * PER)
    centered = values - exact(mean, group_map(0, True))[:1]
    spread = (centered * centered).sum(axis=0, keepdims=True)
    return mean + exact(jnp.broadcast_to(spread, (8, width)), group_map(GROUPS))


def merged_stats(every_ref, count, eps):
    every = every_ref[...]
    average = every.sum(axis=0) / PEERS
    shifted = every - average[None]
    between = (shifted * shifted).sum(axis=0) / PEERS
    var = pltpu.roll(average, 128 - GROUPS, 1) / (count * PER) + between
    lane = lax.broadcasted_iota(jnp.int32, var.shape, 1)
    inverse = jnp.where(lane < GROUPS, lax.rsqrt(var + eps), 0.0)
    spreading = group_map(0, True)
    return exact(average, spreading)[:1], exact(inverse, spreading)[:1]


def exchanged(stats):
    return lax.all_to_all(stats, "space", 0, 0, tiled=True)


def first_stats(latent_ref, out_ref):
    stats = local_stats(latent_ref[...].astype(jnp.float32))
    out_ref[...] = jnp.broadcast_to(stats[None], out_ref.shape)


def prepare(where_ref, every_ref, pair_ref, gain_ref, shift_ref, out_ref, flat_ref):
    core, chip = where_ref[0], where_ref[1]
    count = pair_ref.shape[2]
    mean, inverse = merged_stats(every_ref, count, 1e-05)
    factor = inverse * gain_ref[...]
    token = lax.broadcasted_iota(jnp.int32, (count, 640), 0)
    flat_ref[:, 5760:] = jnp.zeros((2 * count, 128), jnp.bfloat16)
    for row, (holder, which) in enumerate(((1, 1), (0, 0), (1, 0), (0, 1))):
        value = pair_ref[holder, which].astype(jnp.float32)
        value = (value - mean) * factor + shift_ref[...]
        value = value / (1.0 + jnp.exp(-value))
        if row == 0:
            value = jnp.where(chip > 0, value, 0.0)
        if row == 3:
            value = jnp.where(chip < PEERS // 2 - 1, value, 0.0)
        value = value.astype(jnp.bfloat16).astype(jnp.float32)
        shifts = (
            jnp.where(token == 0, 0.0, pltpu.roll(value, 1, 0)),
            value,
            jnp.where(token == count - 1, 0.0, pltpu.roll(value, count - 1, 0)),
        )
        for across, shifted in enumerate(shifts):
            shifted = shifted.astype(jnp.bfloat16)
            for out in range(2):
                down = row - out
                if 0 <= down <= 2:
                    at = (3 * down + across) * 640
                    flat_ref[out * count : (out + 1) * count, at : at + 640] = shifted
    for parity in range(2):

        @pl.when(core == parity)
        def _():
            for index in range(16):
                at = 360 * index + 180 * parity
                low = at // 128 * 128
                wide = flat_ref[:, low : low + 384]
                out_ref[index] = wide[:, at - low : at - low + ROWS]


def time_embed(timestep, time_weight):
    half = TFREQ // 2
    index = jnp.arange(half, dtype=jnp.float32)
    freq = jnp.exp(-math.log(10000.0) * index / half)
    angle = timestep.astype(jnp.float32)[0] * freq
    feats = jnp.concatenate([jnp.cos(angle), jnp.sin(angle)])[None, :]
    return jnp.dot(feats, time_weight, precision=lax.Precision.HIGHEST)


def dot32(a, b):
    return jnp.dot(a, b, preferred_element_type=jnp.float32)


def dot_t(a, b):
    return lax.dot_general(
        a, b, (((1,), (1,)), ((), ())), preferred_element_type=jnp.float32
    )


def conv_near(where_ref, blocks_ref, own_ref, left_ref, right_ref, out_ref):
    x = where_ref[2]
    total = None
    for step, ref in ((0, own_ref), (3, left_ref), (1, right_ref)):
        first = 4 * ((x + step) & 3)
        for z in range(4):
            part = dot32(blocks_ref[first + z], ref[z])
            total = part if total is None else total + part
    out_ref[...] = total


def conv_far(where_ref, blocks_ref, low_ref, high_ref, near_ref, kept_ref, given_ref):
    first = 4 * ((where_ref[2] + 2) & 3)
    total = near_ref[...]
    for z in range(4):
        ref = low_ref if z < 2 else high_ref
        total = total + dot32(blocks_ref[first + z], ref[z % 2])
    count = kept_ref.shape[0]
    kept_ref[...] = jnp.where(where_ref[0] == 0, total[:count], total[count:])
    given_ref[...] = jnp.where(where_ref[0] == 0, total[count:], total[:count])


def middle(kept_ref, other_ref, latent_ref, bias_ref, mid_ref, stats_ref):
    conv = kept_ref[...] + other_ref[...]
    mid = (latent_ref[...].astype(jnp.float32) + conv + bias_ref[...]).astype(jnp.bfloat16)
    mid_ref[...] = mid
    stats = local_stats(mid.astype(jnp.float32))
    stats_ref[...] = jnp.broadcast_to(stats[None], stats_ref.shape)


def project(every_ref, mid_ref, gain_ref, shift_ref, weight_ref, query_ref, fresh_ref):
    mid = mid_ref[...].astype(jnp.float32)
    mean, inverse = merged_stats(every_ref, mid.shape[0], 1e-06)
    normed = ((mid - mean) * (inverse * gain_ref[...]) + shift_ref[...]).astype(jnp.bfloat16)
    query = dot_t(normed, weight_ref[:384])
    lane = lax.broadcasted_iota(jnp.int32, query.shape, 1)
    query = jnp.where(lane < HEADS * HEAD_DIM, query, 0.0).astype(jnp.bfloat16)
    query_ref[...] = query * jnp.bfloat16(1.0 / math.sqrt(HEAD_DIM))
    fresh_ref[...] = dot_t(weight_ref[HEADS * HEAD_DIM :], normed).astype(jnp.bfloat16)


def attend(
    where_ref,
    q_ref,
    other_ref,
    own_ref,
    left_ref,
    right_ref,
    low_ref,
    high_ref,
    fresh_ref,
    out_ref,
    given_ref,
):
    my_z = where_ref[3]
    count = q_ref.shape[0]
    lane = lax.broadcasted_iota(jnp.int32, (2 * count, 128), 1)
    row = lax.broadcasted_iota(jnp.int32, (2 * count, 4 * count), 0)
    block = lax.broadcasted_iota(jnp.int32, (2 * count, 4 * count), 1) // count
    replaced = (row < count) & (block == my_z)
    held = (own_ref, left_ref, right_ref, low_ref, high_ref)
    outs = []
    for head in range(HEADS):
        at = 128 * (head // 2)
        mine = (lane < 64) if head % 2 == 0 else (lane >= 64)
        query = jnp.concatenate(
            [q_ref[:, at : at + 128], other_ref[:, at : at + 128]], axis=0
        )
        query = jnp.where(mine, query.astype(jnp.float32), 0.0).astype(jnp.bfloat16)
        scores = []
        for ref in held:
            keys = [ref[z, at : at + 128] for z in range(ref.shape[0])]
            scores.append(dot32(query, jnp.concatenate(keys, axis=1)))
        scores[0] = jnp.where(replaced, LOW, scores[0])
        fresh = dot32(query[:count], fresh_ref[at : at + 128])
        scores.append(jnp.concatenate([fresh, jnp.full((count, count), LOW, jnp.float32)], axis=0))
        peak = scores[0].max(axis=1, keepdims=True)
        for s in scores[1:]:
            peak = jnp.maximum(peak, s.max(axis=1, keepdims=True))
        total = jnp.zeros((2 * count, 1), jnp.float32)
        mixed = jnp.zeros((2 * count, 128), jnp.float32)
        v_at = HEADS * HEAD_DIM + at
        for s, ref in zip(scores, held + (fresh_ref,), strict=True):
            weights = jnp.exp(s - peak)
            total = total + weights.sum(axis=1, keepdims=True)
            if ref is fresh_ref:
                values = ref[v_at : v_at + 128]
            else:
                values = [ref[z, v_at : v_at + 128] for z in range(ref.shape[0])]
                values = jnp.concatenate(values, axis=1)
            if head == HEADS - 1:
                values = jnp.concatenate([values, jnp.zeros_like(values)], axis=0)
            mixed = mixed + dot_t(weights.astype(jnp.bfloat16), values)
        outs.append((mixed, peak, total))
    last = jnp.where(lane < 64, outs[4][0], 0.0)
    for head in range(HEADS):
        last = jnp.where(lane == 64 + head, outs[head][1], last)
        last = jnp.where(lane == 72 + head, outs[head][2], last)
    tiles = (
        jnp.where(lane < 64, outs[0][0], outs[1][0]),
        jnp.where(lane < 64, outs[2][0], outs[3][0]),
        last,
    )
    for tile, value in enumerate(tiles):
        out_ref[:, 128 * tile : 128 * (tile + 1)] = value[:count]
        given_ref[:, 128 * tile : 128 * (tile + 1)] = value[count:]


def finish(own_ref, other_ref, mid_ref, weight_ref, out_ref):
    count = mid_ref.shape[0]
    lane = lax.broadcasted_iota(jnp.int32, (count, 128), 1)
    factors = []
    for head in range(HEADS):
        peak1 = own_ref[:, 320 + head : 321 + head]
        peak2 = other_ref[:, 320 + head : 321 + head]
        peak = jnp.maximum(peak1, peak2)
        one, two = jnp.exp(peak1 - peak), jnp.exp(peak2 - peak)
        total = own_ref[:, 328 + head : 329 + head] * one
        total = total + other_ref[:, 328 + head : 329 + head] * two
        factors.append((one / total, two / total))
    result = mid_ref[...].astype(jnp.float32)
    for tile in range(3):
        first = factors[2 * tile]
        second = factors[min(2 * tile + 1, HEADS - 1)]
        at = 128 * tile
        mixed = own_ref[:, at : at + 128] * jnp.where(lane < 64, first[0], second[0])
        mixed = mixed + other_ref[:, at : at + 128] * jnp.where(lane < 64, first[1], second[1])
        mixed = mixed.astype(jnp.bfloat16)
        if tile == 2:
            mixed = mixed[:, :HEAD_DIM]
        result = result + dot32(mixed, weight_ref[at : at + mixed.shape[1]])
    out_ref[...] = result.astype(jnp.bfloat16)


def call(kernel, outs, smem, *args, scratch=()):
    return pl.pallas_call(
        kernel,
        out_shape=[jax.ShapeDtypeStruct(shape, dtype) for shape, dtype in outs],
        in_specs=[SMEM] * smem + [VMEM] * (len(args) - smem),
        out_specs=[VMEM] * len(outs),
        scratch_shapes=list(scratch),
        compiler_params=pltpu.CompilerParams(vmem_limit_bytes=40 * 1024 * 1024),
    )(*args)


def on_device(
    latent,
    timestep,
    norm1_gain,
    norm1_shift,
    conv_weight,
    conv_bias,
    time_weight,
    norm2_gain,
    norm2_shift,
    qkv_weight,
    out_weight,
    stale_kv,
):
    tok_dev, width = latent.shape
    feats = qkv_weight.shape[1] // 3
    me = lax.axis_index("space")
    where = jnp.stack([me % 2, me // 2, me // 8, (me // 2) % 4])
    rows = conv_weight.shape[0]
    f32, bf16 = jnp.float32, jnp.bfloat16
    table = ((PEERS, 8, 128), f32)

    weight = jnp.pad(conv_weight, ((0, ROWS - rows), (0, 0)))
    own_w = lax.all_gather(weight, "space", axis=0, axis_index_groups=Z_GROUPS)
    left_w = lax.ppermute(own_w, "space", RIGHT)
    right_w = lax.ppermute(own_w, "space", LEFT)
    outer = lax.ppermute(latent, "space", OUTER)
    (stats1,) = call(first_stats, [table], 0, latent)
    every1 = exchanged(stats1)
    pair = lax.all_gather(
        jnp.stack([latent, outer]), "space", axis=0, axis_index_groups=CORE_GROUPS
    )
    stale = stale_kv.transpose(0, 2, 1).reshape(2 * feats, tok_dev)
    stale, _ = lax.optimization_barrier((stale, own_w))
    own_kv = lax.all_to_all(
        jnp.broadcast_to(stale[None], (4, 2 * feats, tok_dev)),
        "space",
        0,
        0,
        axis_index_groups=Z_GROUPS,
        tiled=True,
    )
    every1, pair, left_w, right_w = lax.optimization_barrier((every1, pair, left_w, right_w))
    low_w = lax.ppermute(left_w[:2], "space", RIGHT)
    high_w = lax.ppermute(right_w[2:], "space", LEFT)
    (blocks,) = call(
        prepare,
        [((16, 2 * tok_dev, ROWS), bf16)],
        1,
        where,
        every1,
        pair,
        norm1_gain[None],
        norm1_shift[None],
        scratch=[pltpu.VMEM((2 * tok_dev, 5760 + 128), bf16)],
    )
    own_kv, _ = lax.optimization_barrier((own_kv, blocks))
    left_kv = lax.ppermute(own_kv, "space", RIGHT)
    right_kv = lax.ppermute(own_kv, "space", LEFT)

    step, _ = lax.optimization_barrier((timestep, blocks))
    bias = (conv_bias + time_embed(step, time_weight)).reshape(1, width)
    (near,) = call(
        conv_near, [((2 * tok_dev, width), f32)], 1, where, blocks, own_w, left_w, right_w
    )
    kept, given = call(
        conv_far, [((tok_dev, width), f32)] * 2, 1, where, blocks, low_w, high_w, near
    )
    other = lax.ppermute(given, "space", SWAP)
    mid, stats2 = call(middle, [((tok_dev, width), bf16), table], 0, kept, other, latent, bias)
    every2 = exchanged(stats2)
    low_kv = lax.ppermute(left_kv[:2], "space", RIGHT)
    high_kv = lax.ppermute(right_kv[2:], "space", LEFT)

    query, fresh = call(
        project,
        [((tok_dev, 384), bf16), ((2 * feats, tok_dev), bf16)],
        0,
        every2,
        mid,
        norm2_gain[None],
        norm2_shift[None],
        qkv_weight.T,
    )
    fresh_kv = fresh.reshape(2, feats, tok_dev).transpose(0, 2, 1)
    mine, theirs = call(
        attend,
        [((tok_dev, 384), f32)] * 2,
        1,
        where,
        query,
        lax.ppermute(query, "space", SWAP),
        own_kv,
        left_kv,
        right_kv,
        low_kv,
        high_kv,
        fresh,
    )
    other = lax.ppermute(theirs, "space", SWAP)
    (result,) = call(finish, [((tok_dev, width), bf16)], 0, mine, other, mid, out_weight)
    return (result, fresh_kv)


def solution(mesh):
    return jax.shard_map(
        on_device,
        mesh=mesh,
        in_specs=(
            P(("batch", "space"), None),
            P("batch"),
            P(),
            P(),
            P("space", None),
            P(),
            P(),
            P(),
            P(),
            P(),
            P(),
            P(None, ("batch", "space"), None),
        ),
        out_specs=(P(("batch", "space"), None), P(None, ("batch", "space"), None)),
        check_vma=False,
    )
```

```python
import math

import jax
import jax.numpy as jnp
from jax import lax
from jax.experimental import pallas as pl
from jax.experimental.pallas import tpu as pltpu
from jax.sharding import PartitionSpec as P

GROUPS = 32
HEADS = 5
HEAD_DIM = 64
TFREQ = 320
PER = 20
PEERS = 32
Z_GROUPS = [[8 * x + 2 * z + c for z in range(4)] for x in range(4) for c in range(2)]
CORE_GROUPS = [[2 * k, 2 * k + 1] for k in range(16)]
RIGHT = [(i, (i + 8) % PEERS) for i in range(PEERS)]
LEFT = [(i, (i + 24) % PEERS) for i in range(PEERS)]
SWAP = [(i, i ^ 1) for i in range(PEERS)]
OUTER = [(i, i - 2) for i in range(2, PEERS, 2)] + [(i, i + 2) for i in range(1, PEERS - 2, 2)]
ROWS = 192
LOW = -1e30
VMEM = pl.BlockSpec(memory_space=pltpu.VMEM)
SMEM = pl.BlockSpec(memory_space=pltpu.SMEM)


def group_map(first, transposed=False):
    shape = (128, 640) if transposed else (640, 128)
    channel = lax.broadcasted_iota(jnp.int32, shape, 1 if transposed else 0)
    low = (lax.broadcasted_iota(jnp.int32, shape, 0 if transposed else 1) - first) * PER
    return ((channel >= low) & (channel < low + PER)).astype(jnp.float32)


def exact(a, b):
    return jnp.dot(
        a, b, precision=lax.Precision.HIGHEST, preferred_element_type=jnp.float32
    )


def local_stats(values):
    count, width = values.shape
    summed = jnp.broadcast_to(values.sum(axis=0, keepdims=True), (8, width))
    mean = exact(summed, group_map(0)) / (count * PER)
    centered = values - exact(mean, group_map(0, True))[:1]
    spread = (centered * centered).sum(axis=0, keepdims=True)
    return mean + exact(jnp.broadcast_to(spread, (8, width)), group_map(GROUPS))


def merged_stats(every_ref, count, eps):
    every = every_ref[...]
    average = every.sum(axis=0) / PEERS
    shifted = every - average[None]
    between = (shifted * shifted).sum(axis=0) / PEERS
    var = pltpu.roll(average, 128 - GROUPS, 1) / (count * PER) + between
    lane = lax.broadcasted_iota(jnp.int32, var.shape, 1)
    inverse = jnp.where(lane < GROUPS, lax.rsqrt(var + eps), 0.0)
    spreading = group_map(0, True)
    return exact(average, spreading)[:1], exact(inverse, spreading)[:1]


def exchanged(stats):
    return lax.all_to_all(stats, "space", 0, 0, tiled=True)


def first_stats(latent_ref, out_ref):
    stats = local_stats(latent_ref[...].astype(jnp.float32))
    out_ref[...] = jnp.broadcast_to(stats[None], out_ref.shape)


def prepare(where_ref, every_ref, pair_ref, gain_ref, shift_ref, out_ref, flat_ref):
    core, chip = where_ref[0], where_ref[1]
    count = pair_ref.shape[2]
    mean, inverse = merged_stats(every_ref, count, 1e-05)
    factor = inverse * gain_ref[...]
    token = lax.broadcasted_iota(jnp.int32, (count, 640), 0)
    flat_ref[:, 5760:] = jnp.zeros((2 * count, 128), jnp.bfloat16)
    for row, (holder, which) in enumerate(((1, 1), (0, 0), (1, 0), (0, 1))):
        value = pair_ref[holder, which].astype(jnp.float32)
        value = (value - mean) * factor + shift_ref[...]
        value = value / (1.0 + jnp.exp(-value))
        if row == 0:
            value = jnp.where(chip > 0, value, 0.0)
        if row == 3:
            value = jnp.where(chip < PEERS // 2 - 1, value, 0.0)
        value = value.astype(jnp.bfloat16).astype(jnp.float32)
        shifts = (
            jnp.where(token == 0, 0.0, pltpu.roll(value, 1, 0)),
            value,
            jnp.where(token == count - 1, 0.0, pltpu.roll(value, count - 1, 0)),
        )
        for across, shifted in enumerate(shifts):
            shifted = shifted.astype(jnp.bfloat16)
            for out in range(2):
                down = row - out
                if 0 <= down <= 2:
                    at = (3 * down + across) * 640
                    flat_ref[out * count : (out + 1) * count, at : at + 640] = shifted
    for parity in range(2):

        @pl.when(core == parity)
        def _():
            for index in range(16):
                at = 360 * index + 180 * parity
                low = at // 128 * 128
                wide = flat_ref[:, low : low + 384]
                out_ref[index] = wide[:, at - low : at - low + ROWS]


def time_embed(timestep, time_weight):
    half = TFREQ // 2
    index = jnp.arange(half, dtype=jnp.float32)
    freq = jnp.exp(-math.log(10000.0) * index / half)
    angle = timestep.astype(jnp.float32)[0] * freq
    feats = jnp.concatenate([jnp.cos(angle), jnp.sin(angle)])[None, :]
    return jnp.dot(feats, time_weight, precision=lax.Precision.HIGHEST)


def dot32(a, b):
    return jnp.dot(a, b, preferred_element_type=jnp.float32)


def dot_t(a, b):
    return lax.dot_general(
        a, b, (((1,), (1,)), ((), ())), preferred_element_type=jnp.float32
    )


def convolve(
    where_ref,
    blocks_ref,
    own_ref,
    left_ref,
    right_ref,
    low_ref,
    high_ref,
    kept_ref,
    given_ref,
    held_ref,
    sems,
):
    core, x = where_ref[0], where_ref[2]
    count = kept_ref.shape[0]
    sources = ((own_ref, 0, 0), (left_ref, 3, 0), (right_ref, 1, 0), (low_ref, 2, 0), (high_ref, 2, 2))
    copies, at = [], 0
    for index, (ref, _, _) in enumerate(sources):
        size = ref.shape[0]
        copy = pltpu.make_async_copy(ref, held_ref.at[at : at + size], sems.at[index])
        copy.start()
        copies.append((copy, at, size))
        at += size
    total = None
    for (_, step, first), (copy, at, size) in zip(sources, copies, strict=True):
        copy.wait()
        base = 4 * ((x + step) & 3) + first
        for z in range(size):
            part = dot32(blocks_ref[base + z], held_ref[at + z])
            total = part if total is None else total + part
    kept_ref[...] = jnp.where(core == 0, total[:count], total[count:])
    given_ref[...] = jnp.where(core == 0, total[count:], total[:count])


def middle(kept_ref, other_ref, latent_ref, bias_ref, mid_ref, stats_ref):
    conv = kept_ref[...] + other_ref[...]
    mid = (latent_ref[...].astype(jnp.float32) + conv + bias_ref[...]).astype(jnp.bfloat16)
    mid_ref[...] = mid
    stats = local_stats(mid.astype(jnp.float32))
    stats_ref[...] = jnp.broadcast_to(stats[None], stats_ref.shape)


def project(
    every_ref, mid_ref, other_ref, gain_ref, shift_ref, weight_ref, query_ref, fresh_ref
):
    count = mid_ref.shape[0]
    mean, inverse = merged_stats(every_ref, count, 1e-06)
    mid = jnp.concatenate([mid_ref[...], other_ref[...]], axis=0).astype(jnp.float32)
    normed = ((mid - mean) * (inverse * gain_ref[...]) + shift_ref[...]).astype(jnp.bfloat16)
    query = dot_t(normed, weight_ref[:384])
    lane = lax.broadcasted_iota(jnp.int32, query.shape, 1)
    query = jnp.where(lane < HEADS * HEAD_DIM, query, 0.0).astype(jnp.bfloat16)
    query_ref[...] = query * jnp.bfloat16(1.0 / math.sqrt(HEAD_DIM))
    fresh_ref[...] = dot_t(weight_ref[HEADS * HEAD_DIM :], normed[:count]).astype(jnp.bfloat16)


def attend(
    where_ref,
    q_ref,
    own_ref,
    left_ref,
    right_ref,
    low_ref,
    high_ref,
    fresh_ref,
    out_ref,
    given_ref,
    held_ref,
    sems,
):
    my_z = where_ref[3]
    count = out_ref.shape[0]
    copies, at = [], 0
    for index, ref in enumerate((own_ref, left_ref, right_ref, low_ref, high_ref)):
        size = ref.shape[0]
        copy = pltpu.make_async_copy(ref, held_ref.at[at : at + size], sems.at[index])
        copy.start()
        copies.append(copy)
        at += size
    lane = lax.broadcasted_iota(jnp.int32, (2 * count, 128), 1)
    row = lax.broadcasted_iota(jnp.int32, (2 * count, 4 * count), 0)
    block = lax.broadcasted_iota(jnp.int32, (2 * count, 4 * count), 1) // count
    replaced = (row < count) & (block == my_z)
    outs = []
    for head in range(HEADS):
        at = 128 * (head // 2)
        mine = (lane < 64) if head % 2 == 0 else (lane >= 64)
        query = q_ref[:, at : at + 128].astype(jnp.float32)
        query = jnp.where(mine, query, 0.0).astype(jnp.bfloat16)
        fresh = dot32(query[:count], fresh_ref[at : at + 128])
        fresh = jnp.concatenate([fresh, jnp.full((count, count), LOW, jnp.float32)], axis=0)
        scores = []
        peak = fresh.max(axis=1, keepdims=True)
        for x in range(4):
            if head == 0:
                copies[x].wait()
                if x == 3:
                    copies[4].wait()
            keys = [held_ref[4 * x + z, at : at + 128] for z in range(4)]
            score = dot32(query, jnp.concatenate(keys, axis=1))
            if x == 0:
                score = jnp.where(replaced, LOW, score)
            peak = jnp.maximum(peak, score.max(axis=1, keepdims=True))
            scores.append(score)
        v_at = HEADS * HEAD_DIM + at
        weights = jnp.exp(fresh - peak)
        total = weights.sum(axis=1, keepdims=True)
        tail = (lambda v: jnp.concatenate([v, jnp.zeros_like(v)], axis=0)) if head == HEADS - 1 else (lambda v: v)
        mixed = dot_t(weights.astype(jnp.bfloat16), tail(fresh_ref[v_at : v_at + 128]))
        for x in range(4):
            weights = jnp.exp(scores[x] - peak)
            total = total + weights.sum(axis=1, keepdims=True)
            values = [held_ref[4 * x + z, v_at : v_at + 128] for z in range(4)]
            values = tail(jnp.concatenate(values, axis=1))
            mixed = mixed + dot_t(weights.astype(jnp.bfloat16), values)
        outs.append((mixed, peak, total))
    last = jnp.where(lane < 64, outs[4][0], 0.0)
    for head in range(HEADS):
        last = jnp.where(lane == 64 + head, outs[head][1], last)
        last = jnp.where(lane == 72 + head, outs[head][2], last)
    tiles = (
        jnp.where(lane < 64, outs[0][0], outs[1][0]),
        jnp.where(lane < 64, outs[2][0], outs[3][0]),
        last,
    )
    for tile, value in enumerate(tiles):
        out_ref[:, 128 * tile : 128 * (tile + 1)] = value[:count]
        given_ref[:, 128 * tile : 128 * (tile + 1)] = value[count:]


def finish(own_ref, other_ref, mid_ref, weight_ref, out_ref):
    count = mid_ref.shape[0]
    lane = lax.broadcasted_iota(jnp.int32, (count, 128), 1)
    factors = []
    for head in range(HEADS):
        peak1 = own_ref[:, 320 + head : 321 + head]
        peak2 = other_ref[:, 320 + head : 321 + head]
        peak = jnp.maximum(peak1, peak2)
        one, two = jnp.exp(peak1 - peak), jnp.exp(peak2 - peak)
        total = own_ref[:, 328 + head : 329 + head] * one
        total = total + other_ref[:, 328 + head : 329 + head] * two
        factors.append((one / total, two / total))
    result = mid_ref[...].astype(jnp.float32)
    for tile in range(3):
        first = factors[2 * tile]
        second = factors[min(2 * tile + 1, HEADS - 1)]
        at = 128 * tile
        mixed = own_ref[:, at : at + 128] * jnp.where(lane < 64, first[0], second[0])
        mixed = mixed + other_ref[:, at : at + 128] * jnp.where(lane < 64, first[1], second[1])
        mixed = mixed.astype(jnp.bfloat16)
        if tile == 2:
            mixed = mixed[:, :HEAD_DIM]
        result = result + dot32(mixed, weight_ref[at : at + mixed.shape[1]])
    out_ref[...] = result.astype(jnp.bfloat16)


def call(kernel, outs, smem, *args, scratch=(), fetched=()):
    return pl.pallas_call(
        kernel,
        out_shape=[jax.ShapeDtypeStruct(shape, dtype) for shape, dtype in outs],
        in_specs=[
            SMEM if i < smem else pl.BlockSpec(memory_space=pl.ANY) if i in fetched else VMEM
            for i in range(len(args))
        ],
        out_specs=[VMEM] * len(outs),
        scratch_shapes=list(scratch),
        compiler_params=pltpu.CompilerParams(vmem_limit_bytes=40 * 1024 * 1024),
    )(*args)


def on_device(
    latent,
    timestep,
    norm1_gain,
    norm1_shift,
    conv_weight,
    conv_bias,
    time_weight,
    norm2_gain,
    norm2_shift,
    qkv_weight,
    out_weight,
    stale_kv,
):
    tok_dev, width = latent.shape
    feats = qkv_weight.shape[1] // 3
    me = lax.axis_index("space")
    where = jnp.stack([me % 2, me // 2, me // 8, (me // 2) % 4])
    rows = conv_weight.shape[0]
    f32, bf16 = jnp.float32, jnp.bfloat16
    table = ((PEERS, 8, 128), f32)

    weight = jnp.pad(conv_weight, ((0, ROWS - rows), (0, 0)))
    own_w = lax.all_gather(weight, "space", axis=0, axis_index_groups=Z_GROUPS)
    left_w = lax.ppermute(own_w, "space", RIGHT)
    right_w = lax.ppermute(own_w, "space", LEFT)
    outer = lax.ppermute(latent, "space", OUTER)
    (stats1,) = call(first_stats, [table], 0, latent)
    every1 = exchanged(stats1)
    pair = lax.all_gather(
        jnp.stack([latent, outer]), "space", axis=0, axis_index_groups=CORE_GROUPS
    )
    stale = stale_kv.transpose(0, 2, 1).reshape(2 * feats, tok_dev)
    stale, _ = lax.optimization_barrier((stale, (left_w,right_w,pair)))
    own_kv = lax.all_to_all(
        jnp.broadcast_to(stale[None], (4, 2 * feats, tok_dev)),
        "space",
        0,
        0,
        axis_index_groups=Z_GROUPS,
        tiled=True,
    )

    low_w = lax.ppermute(left_w[:2], "space", RIGHT)
    high_w = lax.ppermute(right_w[2:], "space", LEFT)
    (blocks,) = call(
        prepare,
        [((16, 2 * tok_dev, ROWS), bf16)],
        1,
        where,
        every1,
        pair,
        norm1_gain[None],
        norm1_shift[None],
        scratch=[pltpu.VMEM((2 * tok_dev, 5760 + 128), bf16)],
    )
    own_kv, _ = lax.optimization_barrier((own_kv, blocks))
    left_kv = lax.ppermute(own_kv, "space", RIGHT)
    right_kv = lax.ppermute(own_kv, "space", LEFT)
    step, _ = lax.optimization_barrier((timestep, blocks))
    bias = (conv_bias + time_embed(step, time_weight)).reshape(1, width)
    kept, given = call(
        convolve,
        [((tok_dev, width), f32)] * 2,
        1,
        where,
        blocks,
        own_w,
        left_w,
        right_w,
        low_w,
        high_w,
        scratch=[pltpu.VMEM((16, ROWS, width), bf16), pltpu.SemaphoreType.DMA((5,))],
        fetched=(2, 3, 4, 5, 6),
    )
    other = lax.ppermute(given, "space", SWAP)
    mid, stats2 = call(middle, [((tok_dev, width), bf16), table], 0, kept, other, latent, bias)
    every2 = exchanged(stats2)
    low_kv = lax.ppermute(left_kv[:2], "space", RIGHT)
    high_kv = lax.ppermute(right_kv[2:], "space", LEFT)
    query, fresh = call(
        project,
        [((2 * tok_dev, 384), bf16), ((2 * feats, tok_dev), bf16)],
        0,
        every2,
        mid,
        lax.ppermute(mid, "space", SWAP),
        norm2_gain[None],
        norm2_shift[None],
        qkv_weight.T,
    )
    fresh_kv = fresh.reshape(2, feats, tok_dev).transpose(0, 2, 1)
    mine, theirs = call(
        attend,
        [((tok_dev, 384), f32)] * 2,
        1,
        where,
        query,
        own_kv,
        left_kv,
        right_kv,
        low_kv,
        high_kv,
        fresh,
        scratch=[pltpu.VMEM((16, 2 * feats, tok_dev), bf16), pltpu.SemaphoreType.DMA((5,))],
        fetched=(2, 3, 4, 5, 6),
    )
    other = lax.ppermute(theirs, "space", SWAP)
    (result,) = call(finish, [((tok_dev, width), bf16)], 0, mine, other, mid, out_weight)
    return (result, fresh_kv)


def solution(mesh):
    return jax.shard_map(
        on_device,
        mesh=mesh,
        in_specs=(
            P(("batch", "space"), None),
            P("batch"),
            P(),
            P(),
            P("space", None),
            P(),
            P(),
            P(),
            P(),
            P(),
            P(),
            P(None, ("batch", "space"), None),
        ),
        out_specs=(P(("batch", "space"), None), P(None, ("batch", "space"), None)),
        check_vma=False,
    )
```

```python
import math

import jax
import jax.numpy as jnp
from jax import lax
from jax.experimental import pallas as pl
from jax.experimental.pallas import tpu as pltpu
from jax.sharding import PartitionSpec as P

GROUPS = 32
HEADS = 5
HEAD_DIM = 64
TFREQ = 320
PER = 20
PEERS = 32
Z_GROUPS = [[8 * x + 2 * z + c for z in range(4)] for x in range(4) for c in range(2)]
RIGHT = [(i, (i + 8) % PEERS) for i in range(PEERS)]
LEFT = [(i, (i + 24) % PEERS) for i in range(PEERS)]
SWAP = [(i, i ^ 1) for i in range(PEERS)]
UP = [(i, i + 1) for i in range(PEERS - 1)]
DOWN = [(i + 1, i) for i in range(PEERS - 1)]
ROWS = 192
CHUNKS = 8
LOW = -1e30
VMEM = pl.BlockSpec(memory_space=pltpu.VMEM)
SMEM = pl.BlockSpec(memory_space=pltpu.SMEM)


def group_map(first, transposed=False):
    shape = (128, 640) if transposed else (640, 128)
    channel = lax.broadcasted_iota(jnp.int32, shape, 1 if transposed else 0)
    low = (lax.broadcasted_iota(jnp.int32, shape, 0 if transposed else 1) - first) * PER
    return ((channel >= low) & (channel < low + PER)).astype(jnp.float32)


def exact(a, b):
    return jnp.dot(
        a, b, precision=lax.Precision.HIGHEST, preferred_element_type=jnp.float32
    )


def local_stats(values):
    count, width = values.shape
    summed = jnp.broadcast_to(values.sum(axis=0, keepdims=True), (8, width))
    mean = exact(summed, group_map(0)) / (count * PER)
    centered = values - exact(mean, group_map(0, True))[:1]
    spread = (centered * centered).sum(axis=0, keepdims=True)
    return mean + exact(jnp.broadcast_to(spread, (8, width)), group_map(GROUPS))


def merged_stats(every_ref, count, eps):
    every = every_ref[...]
    average = every.sum(axis=0) / PEERS
    shifted = every - average[None]
    between = (shifted * shifted).sum(axis=0) / PEERS
    var = pltpu.roll(average, 128 - GROUPS, 1) / (count * PER) + between
    lane = lax.broadcasted_iota(jnp.int32, var.shape, 1)
    inverse = jnp.where(lane < GROUPS, lax.rsqrt(var + eps), 0.0)
    spreading = group_map(0, True)
    return exact(average, spreading)[:1], exact(inverse, spreading)[:1]


def exchanged(stats):
    return lax.all_to_all(stats, "space", 0, 0, tiled=True)


def first_stats(latent_ref, out_ref):
    stats = local_stats(latent_ref[...].astype(jnp.float32))
    out_ref[...] = jnp.broadcast_to(stats[None], out_ref.shape)


def prepare(
    where_ref, every_ref, before_ref, latent_ref, after_ref, gain_ref, shift_ref, out_ref
):
    me = where_ref[0]
    count = latent_ref.shape[0]
    mean, inverse = merged_stats(every_ref, count, 1e-05)
    factor = inverse * gain_ref[...]
    token = lax.broadcasted_iota(jnp.int32, (count, 640), 0)
    for down, ref in enumerate((before_ref, latent_ref, after_ref)):
        value = ref[...].astype(jnp.float32)
        value = (value - mean) * factor + shift_ref[...]
        value = value / (1.0 + jnp.exp(-value))
        if down == 0:
            value = jnp.where(me > 0, value, 0.0)
        if down == 2:
            value = jnp.where(me < PEERS - 1, value, 0.0)
        value = value.astype(jnp.bfloat16).astype(jnp.float32)
        shifts = (
            jnp.where(token == 0, 0.0, pltpu.roll(value, 1, 0)),
            value,
            jnp.where(token == count - 1, 0.0, pltpu.roll(value, count - 1, 0)),
        )
        for across, shifted in enumerate(shifts):
            at = (3 * down + across) * 640
            out_ref[:, at : at + 640] = shifted.astype(jnp.bfloat16)


def time_embed(timestep, time_weight):
    half = TFREQ // 2
    index = jnp.arange(half, dtype=jnp.float32)
    freq = jnp.exp(-math.log(10000.0) * index / half)
    angle = timestep.astype(jnp.float32)[0] * freq
    feats = jnp.concatenate([jnp.cos(angle), jnp.sin(angle)])[None, :]
    return jnp.dot(feats, time_weight, precision=lax.Precision.HIGHEST)


def dot32(a, b):
    return jnp.dot(a, b, preferred_element_type=jnp.float32)


def dot_t(a, b):
    return lax.dot_general(
        a, b, (((1,), (1,)), ((), ())), preferred_element_type=jnp.float32
    )


def convolve(
    unfolded_ref, weight_ref, latent_ref, bias_ref, mid_ref, stats_ref, held_ref, sems
):
    rows = weight_ref.shape[0] // CHUNKS
    copies = []
    for index in range(CHUNKS):
        part = pl.ds(index * rows, rows)
        copy = pltpu.make_async_copy(weight_ref.at[part], held_ref.at[part], sems.at[index])
        copy.start()
        copies.append(copy)
    total = latent_ref[...].astype(jnp.float32) + bias_ref[...]
    conv = None
    for index, copy in enumerate(copies):
        at = index * rows
        copy.wait()
        part = dot32(unfolded_ref[:, at : at + rows], held_ref[at : at + rows])
        conv = part if conv is None else conv + part
    mid = (total + conv).astype(jnp.bfloat16)
    mid_ref[...] = mid
    stats = local_stats(mid.astype(jnp.float32))
    stats_ref[...] = jnp.broadcast_to(stats[None], stats_ref.shape)


def project(
    every_ref, mid_ref, other_ref, gain_ref, shift_ref, weight_ref, query_ref, fresh_ref
):
    count = mid_ref.shape[0]
    mean, inverse = merged_stats(every_ref, count, 1e-06)
    mid = jnp.concatenate([mid_ref[...], other_ref[...]], axis=0).astype(jnp.float32)
    normed = ((mid - mean) * (inverse * gain_ref[...]) + shift_ref[...]).astype(jnp.bfloat16)
    query = dot_t(normed, weight_ref[:384])
    lane = lax.broadcasted_iota(jnp.int32, query.shape, 1)
    query = jnp.where(lane < HEADS * HEAD_DIM, query, 0.0).astype(jnp.bfloat16)
    query_ref[...] = query * jnp.bfloat16(1.0 / math.sqrt(HEAD_DIM))
    fresh_ref[...] = dot_t(weight_ref[HEADS * HEAD_DIM :], normed[:count]).astype(jnp.bfloat16)


def attend(
    where_ref,
    q_ref,
    own_ref,
    left_ref,
    right_ref,
    low_ref,
    high_ref,
    fresh_ref,
    out_ref,
    given_ref,
):
    my_z = where_ref[1]
    count = out_ref.shape[0]
    held = [[(ref, z) for z in range(4)] for ref in (own_ref, left_ref, right_ref)]
    held.append([(low_ref, 0), (low_ref, 1), (high_ref, 0), (high_ref, 1)])
    lane = lax.broadcasted_iota(jnp.int32, (2 * count, 128), 1)
    row = lax.broadcasted_iota(jnp.int32, (2 * count, 4 * count), 0)
    block = lax.broadcasted_iota(jnp.int32, (2 * count, 4 * count), 1) // count
    replaced = (row < count) & (block == my_z)
    outs = []
    for head in range(HEADS):
        at = 128 * (head // 2)
        mine = (lane < 64) if head % 2 == 0 else (lane >= 64)
        query = q_ref[:, at : at + 128].astype(jnp.float32)
        query = jnp.where(mine, query, 0.0).astype(jnp.bfloat16)
        fresh = dot32(query[:count], fresh_ref[at : at + 128])
        fresh = jnp.concatenate([fresh, jnp.full((count, count), LOW, jnp.float32)], axis=0)
        scores = []
        peak = fresh.max(axis=1, keepdims=True)
        for x in range(4):
            keys = [ref[z, at : at + 128] for ref, z in held[x]]
            score = dot32(query, jnp.concatenate(keys, axis=1))
            if x == 0:
                score = jnp.where(replaced, LOW, score)
            peak = jnp.maximum(peak, score.max(axis=1, keepdims=True))
            scores.append(score)
        v_at = HEADS * HEAD_DIM + at
        weights = jnp.exp(fresh - peak)
        total = weights.sum(axis=1, keepdims=True)
        tail = (lambda v: jnp.concatenate([v, jnp.zeros_like(v)], axis=0)) if head == HEADS - 1 else (lambda v: v)
        mixed = dot_t(weights.astype(jnp.bfloat16), tail(fresh_ref[v_at : v_at + 128]))
        for x in range(4):
            weights = jnp.exp(scores[x] - peak)
            total = total + weights.sum(axis=1, keepdims=True)
            values = [ref[z, v_at : v_at + 128] for ref, z in held[x]]
            values = tail(jnp.concatenate(values, axis=1))
            mixed = mixed + dot_t(weights.astype(jnp.bfloat16), values)
        outs.append((mixed, peak, total))
    last = jnp.where(lane < 64, outs[4][0], 0.0)
    for head in range(HEADS):
        last = jnp.where(lane == 64 + head, outs[head][1], last)
        last = jnp.where(lane == 72 + head, outs[head][2], last)
    tiles = (
        jnp.where(lane < 64, outs[0][0], outs[1][0]),
        jnp.where(lane < 64, outs[2][0], outs[3][0]),
        last,
    )
    for tile, value in enumerate(tiles):
        out_ref[:, 128 * tile : 128 * (tile + 1)] = value[:count]
        given_ref[:, 128 * tile : 128 * (tile + 1)] = value[count:]


def finish(own_ref, other_ref, mid_ref, weight_ref, out_ref):
    count = mid_ref.shape[0]
    lane = lax.broadcasted_iota(jnp.int32, (count, 128), 1)
    factors = []
    for head in range(HEADS):
        peak1 = own_ref[:, 320 + head : 321 + head]
        peak2 = other_ref[:, 320 + head : 321 + head]
        peak = jnp.maximum(peak1, peak2)
        one, two = jnp.exp(peak1 - peak), jnp.exp(peak2 - peak)
        total = own_ref[:, 328 + head : 329 + head] * one
        total = total + other_ref[:, 328 + head : 329 + head] * two
        factors.append((one / total, two / total))
    result = mid_ref[...].astype(jnp.float32)
    for tile in range(3):
        first = factors[2 * tile]
        second = factors[min(2 * tile + 1, HEADS - 1)]
        at = 128 * tile
        mixed = own_ref[:, at : at + 128] * jnp.where(lane < 64, first[0], second[0])
        mixed = mixed + other_ref[:, at : at + 128] * jnp.where(lane < 64, first[1], second[1])
        mixed = mixed.astype(jnp.bfloat16)
        if tile == 2:
            mixed = mixed[:, :HEAD_DIM]
        result = result + dot32(mixed, weight_ref[at : at + mixed.shape[1]])
    out_ref[...] = result.astype(jnp.bfloat16)


def call(kernel, outs, smem, *args, scratch=(), fetched=(), mib=32):
    return pl.pallas_call(
        kernel,
        out_shape=[jax.ShapeDtypeStruct(shape, dtype) for shape, dtype in outs],
        in_specs=[
            SMEM if i < smem else pl.BlockSpec(memory_space=pltpu.HBM) if i in fetched else VMEM
            for i in range(len(args))
        ],
        out_specs=[VMEM] * len(outs),
        scratch_shapes=list(scratch),
        compiler_params=pltpu.CompilerParams(vmem_limit_bytes=mib * 1024 * 1024),
    )(*args)


def on_device(
    latent,
    timestep,
    norm1_gain,
    norm1_shift,
    conv_weight,
    conv_bias,
    time_weight,
    norm2_gain,
    norm2_shift,
    qkv_weight,
    out_weight,
    stale_kv,
):
    tok_dev, width = latent.shape
    feats = qkv_weight.shape[1] // 3
    me = lax.axis_index("space")
    where = jnp.stack([me, (me // 2) % 4])
    rows = conv_weight.shape[0]
    f32, bf16 = jnp.float32, jnp.bfloat16
    table = ((PEERS, 8, 128), f32)

    weight = jnp.pad(conv_weight, ((0, ROWS - rows), (0, 0)))
    weight = lax.all_gather(weight, "space", axis=0, tiled=True)

    (stats1,) = call(first_stats, [table], 0, latent)
    every1 = exchanged(stats1)
    before = lax.ppermute(latent, "space", UP)
    after = lax.ppermute(latent, "space", DOWN)
    (unfolded,) = call(
        prepare,
        [((tok_dev, 9 * width), bf16)],
        1,
        where,
        every1,
        before,
        latent,
        after,
        norm1_gain[None],
        norm1_shift[None],
    )
    unfolded = jnp.pad(unfolded.reshape(tok_dev, PEERS, rows), ((0, 0), (0, 0), (0, ROWS - rows)))
    unfolded = unfolded.reshape(tok_dev, PEERS * ROWS)

    stale = stale_kv.transpose(0, 2, 1).reshape(2 * feats, tok_dev)
    own_kv = lax.all_to_all(
        jnp.broadcast_to(stale[None], (4, 2 * feats, tok_dev)),
        "space",
        0,
        0,
        axis_index_groups=Z_GROUPS,
        tiled=True,
    )
    left_kv = lax.ppermute(own_kv, "space", RIGHT)
    right_kv = lax.ppermute(own_kv, "space", LEFT)
    low_kv = lax.ppermute(left_kv[:2], "space", RIGHT)
    high_kv = lax.ppermute(right_kv[2:], "space", LEFT)
    bias = (conv_bias + time_embed(timestep, time_weight)).reshape(1, width)
    unfolded, low_kv, high_kv, bias = lax.optimization_barrier((unfolded, low_kv, high_kv, bias))
    mid, stats2 = call(
        convolve,
        [((tok_dev, width), bf16), table],
        0,
        unfolded,
        weight,
        latent,
        bias,
        scratch=[pltpu.VMEM((PEERS * ROWS, width), bf16), pltpu.SemaphoreType.DMA((CHUNKS,))],
        fetched=(1,),
        mib=56,
    )
    every2 = exchanged(stats2)
    query, fresh = call(
        project,
        [((2 * tok_dev, 384), bf16), ((2 * feats, tok_dev), bf16)],
        0,
        every2,
        mid,
        lax.ppermute(mid, "space", SWAP),
        norm2_gain[None],
        norm2_shift[None],
        qkv_weight.T,
    )
    fresh_kv = fresh.reshape(2, feats, tok_dev).transpose(0, 2, 1)
    mine, theirs = call(
        attend,
        [((tok_dev, 384), f32)] * 2,
        1,
        where,
        query,
        own_kv,
        left_kv,
        right_kv,
        low_kv,
        high_kv,
        fresh,
    )
    other = lax.ppermute(theirs, "space", SWAP)
    (result,) = call(finish, [((tok_dev, width), bf16)], 0, mine, other, mid, out_weight)
    return (result, fresh_kv)


def solution(mesh):
    return jax.shard_map(
        on_device,
        mesh=mesh,
        in_specs=(
            P(("batch", "space"), None),
            P("batch"),
            P(),
            P(),
            P("space", None),
            P(),
            P(),
            P(),
            P(),
            P(),
            P(),
            P(None, ("batch", "space"), None),
        ),
        out_specs=(P(("batch", "space"), None), P(None, ("batch", "space"), None)),
        check_vma=False,
    )
```

```python
import math

import jax
import jax.numpy as jnp
from jax import lax
from jax.experimental import pallas as pl
from jax.experimental.pallas import tpu as pltpu
from jax.sharding import PartitionSpec as P

GROUPS = 32
HEADS = 5
HEAD_DIM = 64
TFREQ = 320
PER = 20
PEERS = 32
Z_GROUPS = [[8 * x + 2 * z + c for z in range(4)] for x in range(4) for c in range(2)]
CORE_GROUPS = [[2 * k, 2 * k + 1] for k in range(16)]
RIGHT = [(i, (i + 8) % PEERS) for i in range(PEERS)]
LEFT = [(i, (i + 24) % PEERS) for i in range(PEERS)]
SWAP = [(i, i ^ 1) for i in range(PEERS)]
OUTER = [(i, i - 2) for i in range(2, PEERS, 2)] + [(i, i + 2) for i in range(1, PEERS - 2, 2)]
ROWS = 192
LOW = -1e30
VMEM = pl.BlockSpec(memory_space=pltpu.VMEM)
SMEM = pl.BlockSpec(memory_space=pltpu.SMEM)


def group_map(first, transposed=False):
    shape = (128, 640) if transposed else (640, 128)
    channel = lax.broadcasted_iota(jnp.int32, shape, 1 if transposed else 0)
    low = (lax.broadcasted_iota(jnp.int32, shape, 0 if transposed else 1) - first) * PER
    return ((channel >= low) & (channel < low + PER)).astype(jnp.float32)


def exact(a, b):
    return jnp.dot(
        a, b, precision=lax.Precision.HIGHEST, preferred_element_type=jnp.float32
    )


def local_stats(values):
    count, width = values.shape
    summed = jnp.broadcast_to(values.sum(axis=0, keepdims=True), (8, width))
    mean = exact(summed, group_map(0)) / (count * PER)
    centered = values - exact(mean, group_map(0, True))[:1]
    spread = (centered * centered).sum(axis=0, keepdims=True)
    return mean + exact(jnp.broadcast_to(spread, (8, width)), group_map(GROUPS))


def merged_stats(every_ref, count, eps):
    every = every_ref[...]
    average = every.sum(axis=0) / PEERS
    shifted = every - average[None]
    between = (shifted * shifted).sum(axis=0) / PEERS
    var = pltpu.roll(average, 128 - GROUPS, 1) / (count * PER) + between
    lane = lax.broadcasted_iota(jnp.int32, var.shape, 1)
    inverse = jnp.where(lane < GROUPS, lax.rsqrt(var + eps), 0.0)
    spreading = group_map(0, True)
    return exact(average, spreading)[:1], exact(inverse, spreading)[:1]


def exchanged(stats):
    return lax.all_to_all(stats, "space", 0, 0, tiled=True)


def first_stats(latent_ref, out_ref):
    stats = local_stats(latent_ref[...].astype(jnp.float32))
    out_ref[...] = jnp.broadcast_to(stats[None], out_ref.shape)


def prepare(where_ref, every_ref, pair_ref, gain_ref, shift_ref, out_ref, flat_ref):
    core, chip = where_ref[0], where_ref[1]
    count = pair_ref.shape[2]
    mean, inverse = merged_stats(every_ref, count, 1e-05)
    factor = inverse * gain_ref[...]
    token = lax.broadcasted_iota(jnp.int32, (count, 640), 0)
    flat_ref[:, 5760:] = jnp.zeros((2 * count, 128), jnp.bfloat16)
    for row, (holder, which) in enumerate(((1, 1), (0, 0), (1, 0), (0, 1))):
        value = pair_ref[holder, which].astype(jnp.float32)
        value = (value - mean) * factor + shift_ref[...]
        value = value / (1.0 + jnp.exp(-value))
        if row == 0:
            value = jnp.where(chip > 0, value, 0.0)
        if row == 3:
            value = jnp.where(chip < PEERS // 2 - 1, value, 0.0)
        value = value.astype(jnp.bfloat16).astype(jnp.float32)
        shifts = (
            jnp.where(token == 0, 0.0, pltpu.roll(value, 1, 0)),
            value,
            jnp.where(token == count - 1, 0.0, pltpu.roll(value, count - 1, 0)),
        )
        for across, shifted in enumerate(shifts):
            shifted = shifted.astype(jnp.bfloat16)
            for out in range(2):
                down = row - out
                if 0 <= down <= 2:
                    at = (3 * down + across) * 640
                    flat_ref[out * count : (out + 1) * count, at : at + 640] = shifted
    for parity in range(2):

        @pl.when(core == parity)
        def _():
            for index in range(16):
                at = 360 * index + 180 * parity
                low = at // 128 * 128
                wide = flat_ref[:, low : low + 384]
                out_ref[index] = wide[:, at - low : at - low + ROWS]


def time_embed(timestep, time_weight):
    half = TFREQ // 2
    index = jnp.arange(half, dtype=jnp.float32)
    freq = jnp.exp(-math.log(10000.0) * index / half)
    angle = timestep.astype(jnp.float32)[0] * freq
    feats = jnp.concatenate([jnp.cos(angle), jnp.sin(angle)])[None, :]
    return jnp.dot(feats, time_weight, precision=lax.Precision.HIGHEST)


def dot32(a, b):
    return jnp.dot(a, b, preferred_element_type=jnp.float32)


def dot_t(a, b):
    return lax.dot_general(
        a, b, (((1,), (1,)), ((), ())), preferred_element_type=jnp.float32
    )


def convolve(
    where_ref,
    blocks_ref,
    own_ref,
    left_ref,
    right_ref,
    far_ref,
    kept_ref,
    given_ref,
    held_ref,
    sems,
):
    core, x = where_ref[0], where_ref[2]
    count = kept_ref.shape[0]
    sources = ((own_ref, 0), (left_ref, 3), (right_ref, 1), (far_ref, 2))
    copies = []
    for index, (ref, _) in enumerate(sources):
        copy = pltpu.make_async_copy(ref, held_ref.at[4 * index : 4 * index + 4], sems.at[index])
        copy.start()
        copies.append(copy)
    total = None
    for index, (_, step) in enumerate(sources):
        copies[index].wait()
        base = 4 * ((x + step) & 3)
        for z in range(4):
            part = dot32(blocks_ref[base + z], held_ref[4 * index + z])
            total = part if total is None else total + part
    kept_ref[...] = jnp.where(core == 0, total[:count], total[count:])
    given_ref[...] = jnp.where(core == 0, total[count:], total[:count])


def middle(kept_ref, other_ref, latent_ref, bias_ref, mid_ref, stats_ref):
    conv = kept_ref[...] + other_ref[...]
    mid = (latent_ref[...].astype(jnp.float32) + conv + bias_ref[...]).astype(jnp.bfloat16)
    mid_ref[...] = mid
    stats = local_stats(mid.astype(jnp.float32))
    stats_ref[...] = jnp.broadcast_to(stats[None], stats_ref.shape)


def project(
    every_ref, mid_ref, other_ref, gain_ref, shift_ref, weight_ref, query_ref, fresh_ref
):
    count = mid_ref.shape[0]
    mean, inverse = merged_stats(every_ref, count, 1e-06)
    mid = jnp.concatenate([mid_ref[...], other_ref[...]], axis=0).astype(jnp.float32)
    normed = ((mid - mean) * (inverse * gain_ref[...]) + shift_ref[...]).astype(jnp.bfloat16)
    query = dot_t(normed, weight_ref[:384])
    lane = lax.broadcasted_iota(jnp.int32, query.shape, 1)
    query = jnp.where(lane < HEADS * HEAD_DIM, query, 0.0).astype(jnp.bfloat16)
    query_ref[...] = query * jnp.bfloat16(1.0 / math.sqrt(HEAD_DIM))
    fresh_ref[...] = dot_t(weight_ref[HEADS * HEAD_DIM :], normed[:count]).astype(jnp.bfloat16)


def attention(q_ref, blocks, replaced, fresh_ref, before):
    count = q_ref.shape[0] // 2
    lane = lax.broadcasted_iota(jnp.int32, (2 * count, 128), 1)
    outs = []
    for head in range(HEADS):
        at = 128 * (head // 2)
        v_at = HEADS * HEAD_DIM + at
        mine = (lane < 64) if head % 2 == 0 else (lane >= 64)
        query = q_ref[:, at : at + 128].astype(jnp.float32)
        query = jnp.where(mine, query, 0.0).astype(jnp.bfloat16)
        last = head == HEADS - 1
        scores = []
        for index, parts in enumerate(blocks):
            keys = [ref[z, at : at + 128] for ref, z in parts]
            score = dot32(query, jnp.concatenate(keys, axis=1))
            if replaced is not None and index == 0:
                score = jnp.where(replaced, LOW, score)
            scores.append(score)
        values = []
        for parts in blocks:
            value = jnp.concatenate([ref[z, v_at : v_at + 128] for ref, z in parts], axis=1)
            values.append(value)
        if fresh_ref is not None:
            score = dot32(query[:count], fresh_ref[at : at + 128])
            score = jnp.concatenate([score, jnp.full((count, count), LOW, jnp.float32)], axis=0)
            scores.append(score)
            values.append(fresh_ref[v_at : v_at + 128])
        peak = scores[0].max(axis=1, keepdims=True)
        for score in scores[1:]:
            peak = jnp.maximum(peak, score.max(axis=1, keepdims=True))
        if before is None:
            total = jnp.zeros((2 * count, 1), jnp.float32)
            mixed = jnp.zeros((2 * count, 128), jnp.float32)
        else:
            held = before[:, 320 + head : 321 + head]
            peak = jnp.maximum(peak, held)
            factor = jnp.exp(held - peak)
            total = before[:, 328 + head : 329 + head] * factor
            mixed = before[:, at : at + 128] * factor
        for score, value in zip(scores, values, strict=True):
            weights = jnp.exp(score - peak)
            total = total + weights.sum(axis=1, keepdims=True)
            if last:
                value = jnp.concatenate([value, jnp.zeros_like(value)], axis=0)
            mixed = mixed + dot_t(weights.astype(jnp.bfloat16), value)
        outs.append((mixed, peak, total))
    stats = jnp.where(lane < 64, outs[4][0], 0.0)
    for head in range(HEADS):
        stats = jnp.where(lane == 64 + head, outs[head][1], stats)
        stats = jnp.where(lane == 72 + head, outs[head][2], stats)
    return (
        jnp.where(lane < 64, outs[0][0], outs[1][0]),
        jnp.where(lane < 64, outs[2][0], outs[3][0]),
        stats,
    )


def attend_near(where_ref, q_ref, own_ref, left_ref, right_ref, fresh_ref, out_ref):
    my_z = where_ref[3]
    count = q_ref.shape[0] // 2
    row = lax.broadcasted_iota(jnp.int32, (2 * count, 4 * count), 0)
    block = lax.broadcasted_iota(jnp.int32, (2 * count, 4 * count), 1) // count
    replaced = (row < count) & (block == my_z)
    blocks = [[(ref, z) for z in range(4)] for ref in (own_ref, left_ref, right_ref)]
    for tile, value in enumerate(attention(q_ref, blocks, replaced, fresh_ref, None)):
        out_ref[:, 128 * tile : 128 * (tile + 1)] = value


def attend_far(q_ref, far_ref, near_ref, out_ref, given_ref):
    count = out_ref.shape[0]
    blocks = [[(far_ref, z) for z in range(4)]]
    for tile, value in enumerate(attention(q_ref, blocks, None, None, near_ref)):
        out_ref[:, 128 * tile : 128 * (tile + 1)] = value[:count]
        given_ref[:, 128 * tile : 128 * (tile + 1)] = value[count:]


def finish(own_ref, other_ref, mid_ref, weight_ref, out_ref):
    count = mid_ref.shape[0]
    lane = lax.broadcasted_iota(jnp.int32, (count, 128), 1)
    factors = []
    for head in range(HEADS):
        peak1 = own_ref[:, 320 + head : 321 + head]
        peak2 = other_ref[:, 320 + head : 321 + head]
        peak = jnp.maximum(peak1, peak2)
        one, two = jnp.exp(peak1 - peak), jnp.exp(peak2 - peak)
        total = own_ref[:, 328 + head : 329 + head] * one
        total = total + other_ref[:, 328 + head : 329 + head] * two
        factors.append((one / total, two / total))
    result = mid_ref[...].astype(jnp.float32)
    for tile in range(3):
        first = factors[2 * tile]
        second = factors[min(2 * tile + 1, HEADS - 1)]
        at = 128 * tile
        mixed = own_ref[:, at : at + 128] * jnp.where(lane < 64, first[0], second[0])
        mixed = mixed + other_ref[:, at : at + 128] * jnp.where(lane < 64, first[1], second[1])
        mixed = mixed.astype(jnp.bfloat16)
        if tile == 2:
            mixed = mixed[:, :HEAD_DIM]
        result = result + dot32(mixed, weight_ref[at : at + mixed.shape[1]])
    out_ref[...] = result.astype(jnp.bfloat16)


def call(kernel, outs, smem, *args, scratch=(), fetched=(), mib=32):
    return pl.pallas_call(
        kernel,
        out_shape=[jax.ShapeDtypeStruct(shape, dtype) for shape, dtype in outs],
        in_specs=[
            SMEM if i < smem else pl.BlockSpec(memory_space=pltpu.HBM) if i in fetched else VMEM
            for i in range(len(args))
        ],
        out_specs=[VMEM] * len(outs),
        scratch_shapes=list(scratch),
        compiler_params=pltpu.CompilerParams(vmem_limit_bytes=mib * 1024 * 1024),
    )(*args)


def on_device(
    latent,
    timestep,
    norm1_gain,
    norm1_shift,
    conv_weight,
    conv_bias,
    time_weight,
    norm2_gain,
    norm2_shift,
    qkv_weight,
    out_weight,
    stale_kv,
):
    tok_dev, width = latent.shape
    feats = qkv_weight.shape[1] // 3
    me = lax.axis_index("space")
    where = jnp.stack([me % 2, me // 2, me // 8, (me // 2) % 4])
    rows = conv_weight.shape[0]
    f32, bf16 = jnp.float32, jnp.bfloat16
    table = ((PEERS, 8, 128), f32)

    weight = jnp.pad(conv_weight, ((0, ROWS - rows), (0, 0)))
    own_w = lax.all_gather(weight, "space", axis=0, axis_index_groups=Z_GROUPS)
    outer = lax.ppermute(latent, "space", OUTER)
    own_w, outer = lax.optimization_barrier((own_w, outer))
    left_w = lax.ppermute(own_w, "space", RIGHT)
    right_w = lax.ppermute(own_w, "space", LEFT)
    (stats1,) = call(first_stats, [table], 0, latent)
    every1 = exchanged(stats1)
    pair = lax.all_gather(
        jnp.stack([latent, outer]), "space", axis=0, axis_index_groups=CORE_GROUPS
    )
    stale = stale_kv.transpose(0, 2, 1).reshape(2 * feats, tok_dev)
    stale, _ = lax.optimization_barrier((stale, (left_w,right_w,pair)))
    own_kv = lax.all_to_all(
        jnp.broadcast_to(stale[None], (4, 2 * feats, tok_dev)),
        "space",
        0,
        0,
        axis_index_groups=Z_GROUPS,
        tiled=True,
    )

    far_w = lax.ppermute(right_w, "space", LEFT)
    (blocks,) = call(
        prepare,
        [((16, 2 * tok_dev, ROWS), bf16)],
        1,
        where,
        every1,
        pair,
        norm1_gain[None],
        norm1_shift[None],
        scratch=[pltpu.VMEM((2 * tok_dev, 5760 + 128), bf16)],
    )
    own_kv, _ = lax.optimization_barrier((own_kv, blocks))
    left_kv = lax.ppermute(own_kv, "space", RIGHT)
    right_kv = lax.ppermute(own_kv, "space", LEFT)
    step, _ = lax.optimization_barrier((timestep, blocks))
    bias = (conv_bias + time_embed(step, time_weight)).reshape(1, width)
    kept, given = call(
        convolve,
        [((tok_dev, width), f32)] * 2,
        1,
        where,
        blocks,
        own_w,
        left_w,
        right_w,
        far_w,
        scratch=[pltpu.VMEM((16, ROWS, width), bf16), pltpu.SemaphoreType.DMA((4,))],
        fetched=(2, 3, 4, 5),
        mib=48,
    )
    other = lax.ppermute(given, "space", SWAP)
    mid, stats2 = call(middle, [((tok_dev, width), bf16), table], 0, kept, other, latent, bias)
    every2 = exchanged(stats2)
    other_mid = lax.ppermute(mid, "space", SWAP)
    sent_kv, _ = lax.optimization_barrier((left_kv, every2))
    far_kv = lax.ppermute(sent_kv, "space", RIGHT)
    query, fresh = call(
        project,
        [((2 * tok_dev, 384), bf16), ((2 * feats, tok_dev), bf16)],
        0,
        every2,
        mid,
        other_mid,
        norm2_gain[None],
        norm2_shift[None],
        qkv_weight.T,
    )
    fresh_kv = fresh.reshape(2, feats, tok_dev).transpose(0, 2, 1)
    (near,) = call(
        attend_near,
        [((2 * tok_dev, 384), f32)],
        1,
        where,
        query,
        own_kv,
        left_kv,
        right_kv,
        fresh,
    )
    mine, theirs = call(attend_far, [((tok_dev, 384), f32)] * 2, 0, query, far_kv, near)
    other = lax.ppermute(theirs, "space", SWAP)
    (result,) = call(finish, [((tok_dev, width), bf16)], 0, mine, other, mid, out_weight)
    return (result, fresh_kv)


def solution(mesh):
    return jax.shard_map(
        on_device,
        mesh=mesh,
        in_specs=(
            P(("batch", "space"), None),
            P("batch"),
            P(),
            P(),
            P("space", None),
            P(),
            P(),
            P(),
            P(),
            P(),
            P(),
            P(None, ("batch", "space"), None),
        ),
        out_specs=(P(("batch", "space"), None), P(None, ("batch", "space"), None)),
        check_vma=False,
    )
```

```python
import math

import jax
import jax.numpy as jnp
from jax import lax
from jax.experimental import pallas as pl
from jax.experimental.pallas import tpu as pltpu
from jax.sharding import PartitionSpec as P

GROUPS = 32
HEADS = 5
HEAD_DIM = 64
TFREQ = 320
PER = 20
PEERS = 32
Z_GROUPS = [[8 * x + 2 * z + c for z in range(4)] for x in range(4) for c in range(2)]
CORE_GROUPS = [[2 * k, 2 * k + 1] for k in range(16)]
RIGHT = [(i, (i + 8) % PEERS) for i in range(PEERS)]
LEFT = [(i, (i + 24) % PEERS) for i in range(PEERS)]
SWAP = [(i, i ^ 1) for i in range(PEERS)]
OUTER = [(i, i - 2) for i in range(2, PEERS, 2)] + [(i, i + 2) for i in range(1, PEERS - 2, 2)]
ROWS = 192
LOW = -1e30
VMEM = pl.BlockSpec(memory_space=pltpu.VMEM)
SMEM = pl.BlockSpec(memory_space=pltpu.SMEM)


def group_map(first, transposed=False):
    shape = (128, 640) if transposed else (640, 128)
    channel = lax.broadcasted_iota(jnp.int32, shape, 1 if transposed else 0)
    low = (lax.broadcasted_iota(jnp.int32, shape, 0 if transposed else 1) - first) * PER
    return ((channel >= low) & (channel < low + PER)).astype(jnp.float32)


def exact(a, b):
    return jnp.dot(
        a, b, precision=lax.Precision.HIGHEST, preferred_element_type=jnp.float32
    )


def local_stats(values):
    count, width = values.shape
    summed = jnp.broadcast_to(values.sum(axis=0, keepdims=True), (8, width))
    mean = exact(summed, group_map(0)) / (count * PER)
    centered = values - exact(mean, group_map(0, True))[:1]
    spread = (centered * centered).sum(axis=0, keepdims=True)
    return mean + exact(jnp.broadcast_to(spread, (8, width)), group_map(GROUPS))


def merged_stats(every_ref, count, eps):
    every = every_ref[...]
    average = every.sum(axis=0) / PEERS
    shifted = every - average[None]
    between = (shifted * shifted).sum(axis=0) / PEERS
    var = pltpu.roll(average, 128 - GROUPS, 1) / (count * PER) + between
    lane = lax.broadcasted_iota(jnp.int32, var.shape, 1)
    inverse = jnp.where(lane < GROUPS, lax.rsqrt(var + eps), 0.0)
    spreading = group_map(0, True)
    return exact(average, spreading)[:1], exact(inverse, spreading)[:1]


def exchanged(stats):
    return lax.all_to_all(stats, "space", 0, 0, tiled=True)


def first_stats(latent_ref, out_ref):
    stats = local_stats(latent_ref[...].astype(jnp.float32))
    out_ref[...] = jnp.broadcast_to(stats[None], out_ref.shape)


def prepare(where_ref, every_ref, pair_ref, gain_ref, shift_ref, out_ref, flat_ref):
    core, chip = where_ref[0], where_ref[1]
    count = pair_ref.shape[2]
    mean, inverse = merged_stats(every_ref, count, 1e-05)
    factor = inverse * gain_ref[...]
    token = lax.broadcasted_iota(jnp.int32, (count, 640), 0)
    flat_ref[:, 5760:] = jnp.zeros((2 * count, 128), jnp.bfloat16)
    for row, (holder, which) in enumerate(((1, 1), (0, 0), (1, 0), (0, 1))):
        value = pair_ref[holder, which].astype(jnp.float32)
        value = (value - mean) * factor + shift_ref[...]
        value = value / (1.0 + jnp.exp(-value))
        if row == 0:
            value = jnp.where(chip > 0, value, 0.0)
        if row == 3:
            value = jnp.where(chip < PEERS // 2 - 1, value, 0.0)
        value = value.astype(jnp.bfloat16).astype(jnp.float32)
        shifts = (
            jnp.where(token == 0, 0.0, pltpu.roll(value, 1, 0)),
            value,
            jnp.where(token == count - 1, 0.0, pltpu.roll(value, count - 1, 0)),
        )
        for across, shifted in enumerate(shifts):
            shifted = shifted.astype(jnp.bfloat16)
            for out in range(2):
                down = row - out
                if 0 <= down <= 2:
                    at = (3 * down + across) * 640
                    flat_ref[out * count : (out + 1) * count, at : at + 640] = shifted
    for parity in range(2):

        @pl.when(core == parity)
        def _():
            for index in range(16):
                at = 360 * index + 180 * parity
                low = at // 128 * 128
                wide = flat_ref[:, low : low + 384]
                out_ref[index] = wide[:, at - low : at - low + ROWS]


def time_embed(timestep, time_weight):
    half = TFREQ // 2
    index = jnp.arange(half, dtype=jnp.float32)
    freq = jnp.exp(-math.log(10000.0) * index / half)
    angle = timestep.astype(jnp.float32)[0] * freq
    feats = jnp.concatenate([jnp.cos(angle), jnp.sin(angle)])[None, :]
    return jnp.dot(feats, time_weight, precision=lax.Precision.HIGHEST)


def dot32(a, b):
    return jnp.dot(a, b, preferred_element_type=jnp.float32)


def dot_t(a, b):
    return lax.dot_general(
        a, b, (((1,), (1,)), ((), ())), preferred_element_type=jnp.float32
    )


def convolve(
    where_ref,
    blocks_ref,
    own_ref,
    left_ref,
    right_ref,
    low_ref,
    high_ref,
    kept_ref,
    given_ref,
    held_ref,
    sems,
):
    core, x = where_ref[0], where_ref[2]
    count = kept_ref.shape[0]
    sources = ((own_ref, 0, 0), (left_ref, 3, 0), (right_ref, 1, 0), (low_ref, 2, 0), (high_ref, 2, 2))
    copies, at = [], 0
    for index, (ref, _, _) in enumerate(sources):
        size = ref.shape[0]
        copy = pltpu.make_async_copy(ref, held_ref.at[at : at + size], sems.at[index])
        copy.start()
        copies.append((copy, at, size))
        at += size
    total = None
    for (_, step, first), (copy, at, size) in zip(sources, copies, strict=True):
        copy.wait()
        base = 4 * ((x + step) & 3) + first
        for z in range(size):
            part = dot32(blocks_ref[base + z], held_ref[at + z])
            total = part if total is None else total + part
    kept_ref[...] = jnp.where(core == 0, total[:count], total[count:])
    given_ref[...] = jnp.where(core == 0, total[count:], total[:count])


def middle(kept_ref, other_ref, latent_ref, bias_ref, mid_ref, stats_ref):
    conv = kept_ref[...] + other_ref[...]
    mid = (latent_ref[...].astype(jnp.float32) + conv + bias_ref[...]).astype(jnp.bfloat16)
    mid_ref[...] = mid
    stats = local_stats(mid.astype(jnp.float32))
    stats_ref[...] = jnp.broadcast_to(stats[None], stats_ref.shape)


def project(
    every_ref, mid_ref, other_ref, gain_ref, shift_ref, weight_ref, query_ref, fresh_ref
):
    count = mid_ref.shape[0]
    mean, inverse = merged_stats(every_ref, count, 1e-06)
    mid = jnp.concatenate([mid_ref[...], other_ref[...]], axis=0).astype(jnp.float32)
    normed = ((mid - mean) * (inverse * gain_ref[...]) + shift_ref[...]).astype(jnp.bfloat16)
    query = dot_t(normed, weight_ref[:384])
    lane = lax.broadcasted_iota(jnp.int32, query.shape, 1)
    query = jnp.where(lane < HEADS * HEAD_DIM, query, 0.0).astype(jnp.bfloat16)
    query_ref[...] = query * jnp.bfloat16(1.0 / math.sqrt(HEAD_DIM))
    fresh_ref[...] = dot_t(weight_ref[HEADS * HEAD_DIM :], normed[:count]).astype(jnp.bfloat16)


def attention(q_ref, blocks, replaced, fresh_ref, before):
    count = q_ref.shape[0] // 2
    lane = lax.broadcasted_iota(jnp.int32, (2 * count, 128), 1)
    outs = []
    for head in range(HEADS):
        at = 128 * (head // 2)
        v_at = HEADS * HEAD_DIM + at
        mine = (lane < 64) if head % 2 == 0 else (lane >= 64)
        query = q_ref[:, at : at + 128].astype(jnp.float32)
        query = jnp.where(mine, query, 0.0).astype(jnp.bfloat16)
        last = head == HEADS - 1
        scores = []
        for index, parts in enumerate(blocks):
            keys = [ref[z, at : at + 128] for ref, z in parts]
            score = dot32(query, jnp.concatenate(keys, axis=1))
            if replaced is not None and index == 0:
                score = jnp.where(replaced, LOW, score)
            scores.append(score)
        values = []
        for parts in blocks:
            value = jnp.concatenate([ref[z, v_at : v_at + 128] for ref, z in parts], axis=1)
            values.append(value)
        if fresh_ref is not None:
            score = dot32(query[:count], fresh_ref[at : at + 128])
            score = jnp.concatenate([score, jnp.full((count, count), LOW, jnp.float32)], axis=0)
            scores.append(score)
            values.append(fresh_ref[v_at : v_at + 128])
        peak = scores[0].max(axis=1, keepdims=True)
        for score in scores[1:]:
            peak = jnp.maximum(peak, score.max(axis=1, keepdims=True))
        if before is None:
            total = jnp.zeros((2 * count, 1), jnp.float32)
            mixed = jnp.zeros((2 * count, 128), jnp.float32)
        else:
            held = before[:, 320 + head : 321 + head]
            peak = jnp.maximum(peak, held)
            factor = jnp.exp(held - peak)
            total = before[:, 328 + head : 329 + head] * factor
            mixed = before[:, at : at + 128] * factor
        for score, value in zip(scores, values, strict=True):
            weights = jnp.exp(score - peak)
            total = total + weights.sum(axis=1, keepdims=True)
            if last:
                value = jnp.concatenate([value, jnp.zeros_like(value)], axis=0)
            mixed = mixed + dot_t(weights.astype(jnp.bfloat16), value)
        outs.append((mixed, peak, total))
    stats = jnp.where(lane < 64, outs[4][0], 0.0)
    for head in range(HEADS):
        stats = jnp.where(lane == 64 + head, outs[head][1], stats)
        stats = jnp.where(lane == 72 + head, outs[head][2], stats)
    return (
        jnp.where(lane < 64, outs[0][0], outs[1][0]),
        jnp.where(lane < 64, outs[2][0], outs[3][0]),
        stats,
    )


def attend_near(where_ref, q_ref, own_ref, left_ref, right_ref, fresh_ref, out_ref):
    my_z = where_ref[3]
    count = q_ref.shape[0] // 2
    row = lax.broadcasted_iota(jnp.int32, (2 * count, 4 * count), 0)
    block = lax.broadcasted_iota(jnp.int32, (2 * count, 4 * count), 1) // count
    replaced = (row < count) & (block == my_z)
    blocks = [[(ref, z) for z in range(4)] for ref in (own_ref, left_ref, right_ref)]
    for tile, value in enumerate(attention(q_ref, blocks, replaced, fresh_ref, None)):
        out_ref[:, 128 * tile : 128 * (tile + 1)] = value


def attend_far(q_ref, low_ref, high_ref, near_ref, out_ref, given_ref):
    count = out_ref.shape[0]
    blocks = [[(low_ref, 0), (low_ref, 1), (high_ref, 0), (high_ref, 1)]]
    for tile, value in enumerate(attention(q_ref, blocks, None, None, near_ref)):
        out_ref[:, 128 * tile : 128 * (tile + 1)] = value[:count]
        given_ref[:, 128 * tile : 128 * (tile + 1)] = value[count:]


def finish(own_ref, other_ref, mid_ref, weight_ref, out_ref):
    count = mid_ref.shape[0]
    lane = lax.broadcasted_iota(jnp.int32, (count, 128), 1)
    factors = []
    for head in range(HEADS):
        peak1 = own_ref[:, 320 + head : 321 + head]
        peak2 = other_ref[:, 320 + head : 321 + head]
        peak = jnp.maximum(peak1, peak2)
        one, two = jnp.exp(peak1 - peak), jnp.exp(peak2 - peak)
        total = own_ref[:, 328 + head : 329 + head] * one
        total = total + other_ref[:, 328 + head : 329 + head] * two
        factors.append((one / total, two / total))
    result = mid_ref[...].astype(jnp.float32)
    for tile in range(3):
        first = factors[2 * tile]
        second = factors[min(2 * tile + 1, HEADS - 1)]
        at = 128 * tile
        mixed = own_ref[:, at : at + 128] * jnp.where(lane < 64, first[0], second[0])
        mixed = mixed + other_ref[:, at : at + 128] * jnp.where(lane < 64, first[1], second[1])
        mixed = mixed.astype(jnp.bfloat16)
        if tile == 2:
            mixed = mixed[:, :HEAD_DIM]
        result = result + dot32(mixed, weight_ref[at : at + mixed.shape[1]])
    out_ref[...] = result.astype(jnp.bfloat16)


def call(kernel, outs, smem, *args, scratch=(), fetched=()):
    return pl.pallas_call(
        kernel,
        out_shape=[jax.ShapeDtypeStruct(shape, dtype) for shape, dtype in outs],
        in_specs=[
            SMEM if i < smem else pl.BlockSpec(memory_space=pl.ANY) if i in fetched else VMEM
            for i in range(len(args))
        ],
        out_specs=[VMEM] * len(outs),
        scratch_shapes=list(scratch),
        compiler_params=pltpu.CompilerParams(vmem_limit_bytes=40 * 1024 * 1024),
    )(*args)


def on_device(
    latent,
    timestep,
    norm1_gain,
    norm1_shift,
    conv_weight,
    conv_bias,
    time_weight,
    norm2_gain,
    norm2_shift,
    qkv_weight,
    out_weight,
    stale_kv,
):
    tok_dev, width = latent.shape
    feats = qkv_weight.shape[1] // 3
    me = lax.axis_index("space")
    where = jnp.stack([me % 2, me // 2, me // 8, (me // 2) % 4])
    rows = conv_weight.shape[0]
    f32, bf16 = jnp.float32, jnp.bfloat16
    table = ((PEERS, 8, 128), f32)

    weight = jnp.pad(conv_weight, ((0, ROWS - rows), (0, 0)))
    own_w = lax.all_gather(weight, "space", axis=0, axis_index_groups=Z_GROUPS)
    left_w = lax.ppermute(own_w, "space", RIGHT)
    right_w = lax.ppermute(own_w, "space", LEFT)
    outer = lax.ppermute(latent, "space", OUTER)
    (stats1,) = call(first_stats, [table], 0, latent)
    every1 = exchanged(stats1)
    pair = lax.all_gather(
        jnp.stack([latent, outer]), "space", axis=0, axis_index_groups=CORE_GROUPS
    )
    stale = stale_kv.transpose(0, 2, 1).reshape(2 * feats, tok_dev)
    stale, _ = lax.optimization_barrier((stale, own_w))
    own_kv = lax.all_gather(stale, "space", axis=0, axis_index_groups=Z_GROUPS)
    low_w = lax.ppermute(left_w[:2], "space", RIGHT)
    high_w = lax.ppermute(right_w[2:], "space", LEFT)
    (blocks,) = call(
        prepare,
        [((16, 2 * tok_dev, ROWS), bf16)],
        1,
        where,
        every1,
        pair,
        norm1_gain[None],
        norm1_shift[None],
        scratch=[pltpu.VMEM((2 * tok_dev, 5760 + 128), bf16)],
    )
    own_kv, _ = lax.optimization_barrier((own_kv, blocks))
    left_kv = lax.ppermute(own_kv, "space", RIGHT)
    right_kv = lax.ppermute(own_kv, "space", LEFT)
    step, _ = lax.optimization_barrier((timestep, blocks))
    bias = (conv_bias + time_embed(step, time_weight)).reshape(1, width)
    kept, given = call(
        convolve,
        [((tok_dev, width), f32)] * 2,
        1,
        where,
        blocks,
        own_w,
        left_w,
        right_w,
        low_w,
        high_w,
        scratch=[pltpu.VMEM((16, ROWS, width), bf16), pltpu.SemaphoreType.DMA((5,))],
        fetched=(2, 3, 4, 5, 6),
    )
    other = lax.ppermute(given, "space", SWAP)
    mid, stats2 = call(middle, [((tok_dev, width), bf16), table], 0, kept, other, latent, bias)
    every2 = exchanged(stats2)
    low_kv = lax.ppermute(left_kv[:2], "space", RIGHT)
    high_kv = lax.ppermute(right_kv[2:], "space", LEFT)
    query, fresh = call(
        project,
        [((2 * tok_dev, 384), bf16), ((2 * feats, tok_dev), bf16)],
        0,
        every2,
        mid,
        lax.ppermute(mid, "space", SWAP),
        norm2_gain[None],
        norm2_shift[None],
        qkv_weight.T,
    )
    fresh_kv = fresh.reshape(2, feats, tok_dev).transpose(0, 2, 1)
    (near,) = call(
        attend_near,
        [((2 * tok_dev, 384), f32)],
        1,
        where,
        query,
        own_kv,
        left_kv,
        right_kv,
        fresh,
    )
    mine, theirs = call(
        attend_far, [((tok_dev, 384), f32)] * 2, 0, query, low_kv, high_kv, near
    )
    other = lax.ppermute(theirs, "space", SWAP)
    (result,) = call(finish, [((tok_dev, width), bf16)], 0, mine, other, mid, out_weight)
    return (result, fresh_kv)


def solution(mesh):
    return jax.shard_map(
        on_device,
        mesh=mesh,
        in_specs=(
            P(("batch", "space"), None),
            P("batch"),
            P(),
            P(),
            P("space", None),
            P(),
            P(),
            P(),
            P(),
            P(),
            P(),
            P(None, ("batch", "space"), None),
        ),
        out_specs=(P(("batch", "space"), None), P(None, ("batch", "space"), None)),
        check_vma=False,
    )
```

```python
import math

import jax
import jax.numpy as jnp
from jax import lax
from jax.experimental import pallas as pl
from jax.experimental.pallas import tpu as pltpu
from jax.sharding import PartitionSpec as P

GROUPS = 32
HEADS = 5
HEAD_DIM = 64
TFREQ = 320
PER = 20
PEERS = 32
Z_GROUPS = [[8 * x + 2 * z + c for z in range(4)] for x in range(4) for c in range(2)]
CORE_GROUPS = [[2 * k, 2 * k + 1] for k in range(16)]
RIGHT = [(i, (i + 8) % PEERS) for i in range(PEERS)]
LEFT = [(i, (i + 24) % PEERS) for i in range(PEERS)]
SWAP = [(i, i ^ 1) for i in range(PEERS)]
OUTER = [(i, i - 2) for i in range(2, PEERS, 2)] + [(i, i + 2) for i in range(1, PEERS - 2, 2)]
ROWS = 192
LOW = -1e30
VMEM = pl.BlockSpec(memory_space=pltpu.VMEM)
SMEM = pl.BlockSpec(memory_space=pltpu.SMEM)


def group_map(first, transposed=False):
    shape = (128, 640) if transposed else (640, 128)
    channel = lax.broadcasted_iota(jnp.int32, shape, 1 if transposed else 0)
    low = (lax.broadcasted_iota(jnp.int32, shape, 0 if transposed else 1) - first) * PER
    return ((channel >= low) & (channel < low + PER)).astype(jnp.float32)


def exact(a, b):
    return jnp.dot(
        a, b, precision=lax.Precision.HIGHEST, preferred_element_type=jnp.float32
    )


def local_stats(values):
    count, width = values.shape
    summed = jnp.broadcast_to(values.sum(axis=0, keepdims=True), (8, width))
    mean = exact(summed, group_map(0)) / (count * PER)
    centered = values - exact(mean, group_map(0, True))[:1]
    spread = (centered * centered).sum(axis=0, keepdims=True)
    return mean + exact(jnp.broadcast_to(spread, (8, width)), group_map(GROUPS))


def merged_stats(every_ref, count, eps):
    every = every_ref[...]
    average = every.sum(axis=0) / PEERS
    shifted = every - average[None]
    between = (shifted * shifted).sum(axis=0) / PEERS
    var = pltpu.roll(average, 128 - GROUPS, 1) / (count * PER) + between
    lane = lax.broadcasted_iota(jnp.int32, var.shape, 1)
    inverse = jnp.where(lane < GROUPS, lax.rsqrt(var + eps), 0.0)
    spreading = group_map(0, True)
    return exact(average, spreading)[:1], exact(inverse, spreading)[:1]


def exchanged(stats):
    return lax.all_to_all(stats, "space", 0, 0, tiled=True)


def first_stats(latent_ref, out_ref):
    stats = local_stats(latent_ref[...].astype(jnp.float32))
    out_ref[...] = jnp.broadcast_to(stats[None], out_ref.shape)


def prepare(where_ref, every_ref, pair_ref, gain_ref, shift_ref, out_ref, flat_ref):
    core, chip = where_ref[0], where_ref[1]
    count = pair_ref.shape[2]
    mean, inverse = merged_stats(every_ref, count, 1e-05)
    factor = inverse * gain_ref[...]
    token = lax.broadcasted_iota(jnp.int32, (count, 640), 0)
    flat_ref[:, 5760:] = jnp.zeros((2 * count, 128), jnp.bfloat16)
    for row, (holder, which) in enumerate(((1, 1), (0, 0), (1, 0), (0, 1))):
        value = pair_ref[holder, which].astype(jnp.float32)
        value = (value - mean) * factor + shift_ref[...]
        value = value / (1.0 + jnp.exp(-value))
        if row == 0:
            value = jnp.where(chip > 0, value, 0.0)
        if row == 3:
            value = jnp.where(chip < PEERS // 2 - 1, value, 0.0)
        value = value.astype(jnp.bfloat16).astype(jnp.float32)
        shifts = (
            jnp.where(token == 0, 0.0, pltpu.roll(value, 1, 0)),
            value,
            jnp.where(token == count - 1, 0.0, pltpu.roll(value, count - 1, 0)),
        )
        for across, shifted in enumerate(shifts):
            shifted = shifted.astype(jnp.bfloat16)
            for out in range(2):
                down = row - out
                if 0 <= down <= 2:
                    at = (3 * down + across) * 640
                    flat_ref[out * count : (out + 1) * count, at : at + 640] = shifted
    for parity in range(2):

        @pl.when(core == parity)
        def _():
            for index in range(16):
                at = 360 * index + 180 * parity
                low = at // 128 * 128
                wide = flat_ref[:, low : low + 384]
                out_ref[index] = wide[:, at - low : at - low + ROWS]


def time_embed(timestep, time_weight):
    half = TFREQ // 2
    index = jnp.arange(half, dtype=jnp.float32)
    freq = jnp.exp(-math.log(10000.0) * index / half)
    angle = timestep.astype(jnp.float32)[0] * freq
    feats = jnp.concatenate([jnp.cos(angle), jnp.sin(angle)])[None, :]
    return jnp.dot(feats, time_weight, precision=lax.Precision.HIGHEST)


def dot32(a, b):
    return jnp.dot(a, b, preferred_element_type=jnp.float32)


def dot_t(a, b):
    return lax.dot_general(
        a, b, (((1,), (1,)), ((), ())), preferred_element_type=jnp.float32
    )


def convolve(
    where_ref,
    blocks_ref,
    own_ref,
    left_ref,
    right_ref,
    low_ref,
    high_ref,
    kept_ref,
    given_ref,
    held_ref,
    sems,
):
    core, x = where_ref[0], where_ref[2]
    count = kept_ref.shape[0]
    sources = ((own_ref, 0, 0), (left_ref, 3, 0), (right_ref, 1, 0), (low_ref, 2, 0), (high_ref, 2, 2))
    copies, at = [], 0
    for index, (ref, _, _) in enumerate(sources):
        size = ref.shape[0]
        copy = pltpu.make_async_copy(ref, held_ref.at[at : at + size], sems.at[index])
        copy.start()
        copies.append((copy, at, size))
        at += size
    total = None
    for (_, step, first), (copy, at, size) in zip(sources, copies, strict=True):
        copy.wait()
        base = 4 * ((x + step) & 3) + first
        for z in range(size):
            part = dot32(blocks_ref[base + z], held_ref[at + z])
            total = part if total is None else total + part
    kept_ref[...] = jnp.where(core == 0, total[:count], total[count:])
    given_ref[...] = jnp.where(core == 0, total[count:], total[:count])


def middle(kept_ref, other_ref, latent_ref, bias_ref, mid_ref, stats_ref):
    conv = kept_ref[...] + other_ref[...]
    mid = (latent_ref[...].astype(jnp.float32) + conv + bias_ref[...]).astype(jnp.bfloat16)
    mid_ref[...] = mid
    stats = local_stats(mid.astype(jnp.float32))
    stats_ref[...] = jnp.broadcast_to(stats[None], stats_ref.shape)


def project(
    every_ref, mid_ref, other_ref, gain_ref, shift_ref, weight_ref, query_ref, fresh_ref, kept_ref
):
    count = mid_ref.shape[0]
    mean, inverse = merged_stats(every_ref, count, 1e-06)
    mid = jnp.concatenate([mid_ref[...], other_ref[...]], axis=0).astype(jnp.float32)
    normed = ((mid - mean) * (inverse * gain_ref[...]) + shift_ref[...]).astype(jnp.bfloat16)
    query = dot_t(normed, weight_ref[:384])
    lane = lax.broadcasted_iota(jnp.int32, query.shape, 1)
    query = jnp.where(lane < HEADS * HEAD_DIM, query, 0.0).astype(jnp.bfloat16)
    query_ref[...] = query * jnp.bfloat16(1.0 / math.sqrt(HEAD_DIM))
    fresh = dot_t(weight_ref[HEADS * HEAD_DIM :], normed[:count]).astype(jnp.bfloat16)
    fresh_ref[...] = fresh
    kept_ref[...] = fresh


def attention(q_ref, blocks, replaced, fresh_ref, before):
    count = q_ref.shape[0] // 2
    lane = lax.broadcasted_iota(jnp.int32, (2 * count, 128), 1)
    outs = []
    for head in range(HEADS):
        at = 128 * (head // 2)
        v_at = HEADS * HEAD_DIM + at
        mine = (lane < 64) if head % 2 == 0 else (lane >= 64)
        query = q_ref[:, at : at + 128].astype(jnp.float32)
        query = jnp.where(mine, query, 0.0).astype(jnp.bfloat16)
        last = head == HEADS - 1
        scores = []
        for index, parts in enumerate(blocks):
            keys = [ref[z, at : at + 128] for ref, z in parts]
            score = dot32(query, jnp.concatenate(keys, axis=1))
            if replaced is not None and index == 0:
                score = jnp.where(replaced, LOW, score)
            scores.append(score)
        values = []
        for parts in blocks:
            value = jnp.concatenate([ref[z, v_at : v_at + 128] for ref, z in parts], axis=1)
            values.append(value)
        if fresh_ref is not None:
            score = dot32(query[:count], fresh_ref[at : at + 128])
            score = jnp.concatenate([score, jnp.full((count, count), LOW, jnp.float32)], axis=0)
            scores.append(score)
            values.append(fresh_ref[v_at : v_at + 128])
        peak = scores[0].max(axis=1, keepdims=True)
        for score in scores[1:]:
            peak = jnp.maximum(peak, score.max(axis=1, keepdims=True))
        if before is None:
            total = jnp.zeros((2 * count, 1), jnp.float32)
            mixed = jnp.zeros((2 * count, 128), jnp.float32)
        else:
            held = before[:, 320 + head : 321 + head]
            peak = jnp.maximum(peak, held)
            factor = jnp.exp(held - peak)
            total = before[:, 328 + head : 329 + head] * factor
            mixed = before[:, at : at + 128] * factor
        for score, value in zip(scores, values, strict=True):
            weights = jnp.exp(score - peak)
            total = total + weights.sum(axis=1, keepdims=True)
            if last:
                value = jnp.concatenate([value, jnp.zeros_like(value)], axis=0)
            mixed = mixed + dot_t(weights.astype(jnp.bfloat16), value)
        outs.append((mixed, peak, total))
    stats = jnp.where(lane < 64, outs[4][0], 0.0)
    for head in range(HEADS):
        stats = jnp.where(lane == 64 + head, outs[head][1], stats)
        stats = jnp.where(lane == 72 + head, outs[head][2], stats)
    return (
        jnp.where(lane < 64, outs[0][0], outs[1][0]),
        jnp.where(lane < 64, outs[2][0], outs[3][0]),
        stats,
    )


def attend_near(where_ref, q_ref, own_ref, left_ref, right_ref, fresh_ref, out_ref):
    my_z = where_ref[3]
    count = q_ref.shape[0] // 2
    row = lax.broadcasted_iota(jnp.int32, (2 * count, 4 * count), 0)
    block = lax.broadcasted_iota(jnp.int32, (2 * count, 4 * count), 1) // count
    replaced = (row < count) & (block == my_z)
    blocks = [[(ref, z) for z in range(4)] for ref in (own_ref, left_ref, right_ref)]
    for tile, value in enumerate(attention(q_ref, blocks, replaced, fresh_ref, None)):
        out_ref[:, 128 * tile : 128 * (tile + 1)] = value


def attend_far(q_ref, far_ref, near_ref, out_ref, given_ref):
    count = out_ref.shape[0]
    blocks = [[(far_ref, z) for z in range(4)]]
    for tile, value in enumerate(attention(q_ref, blocks, None, None, near_ref)):
        out_ref[:, 128 * tile : 128 * (tile + 1)] = value[:count]
        given_ref[:, 128 * tile : 128 * (tile + 1)] = value[count:]


def finish(own_ref, other_ref, mid_ref, weight_ref, out_ref):
    count = mid_ref.shape[0]
    lane = lax.broadcasted_iota(jnp.int32, (count, 128), 1)
    factors = []
    for head in range(HEADS):
        peak1 = own_ref[:, 320 + head : 321 + head]
        peak2 = other_ref[:, 320 + head : 321 + head]
        peak = jnp.maximum(peak1, peak2)
        one, two = jnp.exp(peak1 - peak), jnp.exp(peak2 - peak)
        total = own_ref[:, 328 + head : 329 + head] * one
        total = total + other_ref[:, 328 + head : 329 + head] * two
        factors.append((one / total, two / total))
    result = mid_ref[...].astype(jnp.float32)
    for tile in range(3):
        first = factors[2 * tile]
        second = factors[min(2 * tile + 1, HEADS - 1)]
        at = 128 * tile
        mixed = own_ref[:, at : at + 128] * jnp.where(lane < 64, first[0], second[0])
        mixed = mixed + other_ref[:, at : at + 128] * jnp.where(lane < 64, first[1], second[1])
        mixed = mixed.astype(jnp.bfloat16)
        if tile == 2:
            mixed = mixed[:, :HEAD_DIM]
        result = result + dot32(mixed, weight_ref[at : at + mixed.shape[1]])
    out_ref[...] = result.astype(jnp.bfloat16)


def call(kernel, outs, smem, *args, scratch=(), fetched=(), cost=None):
    return pl.pallas_call(
        kernel,
        out_shape=[jax.ShapeDtypeStruct(shape, dtype) for shape, dtype in outs],
        in_specs=[
            SMEM if i < smem else pl.BlockSpec(memory_space=pl.ANY) if i in fetched else VMEM
            for i in range(len(args))
        ],
        out_specs=[VMEM] * len(outs),
        scratch_shapes=list(scratch),
        cost_estimate=cost,
        compiler_params=pltpu.CompilerParams(vmem_limit_bytes=40 * 1024 * 1024),
    )(*args)


def on_device(
    latent,
    timestep,
    norm1_gain,
    norm1_shift,
    conv_weight,
    conv_bias,
    time_weight,
    norm2_gain,
    norm2_shift,
    qkv_weight,
    out_weight,
    stale_kv,
):
    tok_dev, width = latent.shape
    feats = qkv_weight.shape[1] // 3
    me = lax.axis_index("space")
    where = jnp.stack([me % 2, me // 2, me // 8, (me // 2) % 4])
    rows = conv_weight.shape[0]
    f32, bf16 = jnp.float32, jnp.bfloat16
    table = ((PEERS, 8, 128), f32)

    weight = jnp.pad(conv_weight, ((0, ROWS - rows), (0, 0)))
    own_w = lax.all_gather(weight, "space", axis=0, axis_index_groups=Z_GROUPS)
    left_w = lax.ppermute(own_w, "space", RIGHT)
    right_w = lax.ppermute(own_w, "space", LEFT)
    outer = lax.ppermute(latent, "space", OUTER)
    (stats1,) = call(first_stats, [table], 0, latent)
    every1 = exchanged(stats1)
    pair = lax.all_gather(
        jnp.stack([latent, outer]), "space", axis=0, axis_index_groups=CORE_GROUPS
    )
    stale = stale_kv.transpose(0, 2, 1).reshape(2 * feats, tok_dev)
    stale, _ = lax.optimization_barrier((stale, own_w))
    own_kv = lax.all_gather(stale, "space", axis=0, axis_index_groups=Z_GROUPS)
    low_w = lax.ppermute(left_w[:2], "space", RIGHT)
    high_w = lax.ppermute(right_w[2:], "space", LEFT)
    (blocks,) = call(
        prepare,
        [((16, 2 * tok_dev, ROWS), bf16)],
        1,
        where,
        every1,
        pair,
        norm1_gain[None],
        norm1_shift[None],
        scratch=[pltpu.VMEM((2 * tok_dev, 5760 + 128), bf16)],
    )
    own_kv, _ = lax.optimization_barrier((own_kv, blocks))
    left_kv = lax.ppermute(own_kv, "space", RIGHT)
    right_kv = lax.ppermute(own_kv, "space", LEFT)
    step, _ = lax.optimization_barrier((timestep, blocks))
    bias = (conv_bias + time_embed(step, time_weight)).reshape(1, width)
    kept, given = call(
        convolve,
        [((tok_dev, width), f32)] * 2,
        1,
        where,
        blocks,
        own_w,
        left_w,
        right_w,
        low_w,
        high_w,
        scratch=[pltpu.VMEM((16, ROWS, width), bf16), pltpu.SemaphoreType.DMA((5,))],
        fetched=(2, 3, 4, 5, 6),
    )
    other = lax.ppermute(given, "space", SWAP)
    mid, stats2 = call(middle, [((tok_dev, width), bf16), table], 0, kept, other, latent, bias)
    every2 = exchanged(stats2)
    far_kv = lax.ppermute(left_kv, "space", RIGHT)
    query, fresh, kept_kv = call(
        project,
        [((2 * tok_dev, 384), bf16)] + [((2 * feats, tok_dev), bf16)] * 2,
        0,
        every2,
        mid,
        lax.ppermute(mid, "space", SWAP),
        norm2_gain[None],
        norm2_shift[None],
        qkv_weight.T,
    )
    fresh_kv = kept_kv.reshape(2, feats, tok_dev).transpose(0, 2, 1)
    (near,) = call(
        attend_near,
        [((2 * tok_dev, 384), f32)],
        1,
        where,
        query,
        own_kv,
        left_kv,
        right_kv,
        fresh,
        cost=pl.CostEstimate(flops=2000000000, transcendentals=2 * 10**6, bytes_accessed=3 * 10**6),
    )
    mine, theirs = call(
        attend_far, [((tok_dev, 384), f32)] * 2, 0, query, far_kv, near
    )
    other = lax.ppermute(theirs, "space", SWAP)
    (result,) = call(finish, [((tok_dev, width), bf16)], 0, mine, other, mid, out_weight)
    return (result, fresh_kv)


def solution(mesh):
    return jax.shard_map(
        on_device,
        mesh=mesh,
        in_specs=(
            P(("batch", "space"), None),
            P("batch"),
            P(),
            P(),
            P("space", None),
            P(),
            P(),
            P(),
            P(),
            P(),
            P(),
            P(None, ("batch", "space"), None),
        ),
        out_specs=(P(("batch", "space"), None), P(None, ("batch", "space"), None)),
        check_vma=False,
    )
```

```python
import math

import jax
import jax.numpy as jnp
from jax import lax
from jax.experimental import pallas as pl
from jax.experimental.pallas import tpu as pltpu
from jax.sharding import PartitionSpec as P

GROUPS = 32
HEADS = 5
HEAD_DIM = 64
TFREQ = 320
PER = 20
PEERS = 32
Z_GROUPS = [[8 * x + 2 * z + c for z in range(4)] for x in range(4) for c in range(2)]
CORE_GROUPS = [[2 * k, 2 * k + 1] for k in range(16)]
RIGHT = [(i, (i + 8) % PEERS) for i in range(PEERS)]
LEFT = [(i, (i + 24) % PEERS) for i in range(PEERS)]
SWAP = [(i, i ^ 1) for i in range(PEERS)]
OUTER = [(i, i - 2) for i in range(2, PEERS, 2)] + [(i, i + 2) for i in range(1, PEERS - 2, 2)]
ROWS = 192
LOW = -1e30
VMEM = pl.BlockSpec(memory_space=pltpu.VMEM)
SMEM = pl.BlockSpec(memory_space=pltpu.SMEM)


def group_map(first, transposed=False):
    shape = (128, 640) if transposed else (640, 128)
    channel = lax.broadcasted_iota(jnp.int32, shape, 1 if transposed else 0)
    low = (lax.broadcasted_iota(jnp.int32, shape, 0 if transposed else 1) - first) * PER
    return ((channel >= low) & (channel < low + PER)).astype(jnp.float32)


def exact(a, b):
    return jnp.dot(
        a, b, precision=lax.Precision.HIGHEST, preferred_element_type=jnp.float32
    )


def local_stats(values):
    count, width = values.shape
    summed = jnp.broadcast_to(values.sum(axis=0, keepdims=True), (8, width))
    mean = exact(summed, group_map(0)) / (count * PER)
    centered = values - exact(mean, group_map(0, True))[:1]
    spread = (centered * centered).sum(axis=0, keepdims=True)
    return mean + exact(jnp.broadcast_to(spread, (8, width)), group_map(GROUPS))


def merged_stats(every_ref, count, eps):
    every = every_ref[...]
    average = every.sum(axis=0) / PEERS
    shifted = every - average[None]
    between = (shifted * shifted).sum(axis=0) / PEERS
    var = pltpu.roll(average, 128 - GROUPS, 1) / (count * PER) + between
    lane = lax.broadcasted_iota(jnp.int32, var.shape, 1)
    inverse = jnp.where(lane < GROUPS, lax.rsqrt(var + eps), 0.0)
    spreading = group_map(0, True)
    return exact(average, spreading)[:1], exact(inverse, spreading)[:1]


def exchanged(stats):
    return lax.all_to_all(stats, "space", 0, 0, tiled=True)


def first_stats(latent_ref, out_ref):
    stats = local_stats(latent_ref[...].astype(jnp.float32))
    out_ref[...] = jnp.broadcast_to(stats[None], out_ref.shape)


def prepare(where_ref, every_ref, pair_ref, gain_ref, shift_ref, out_ref, flat_ref):
    core, chip = where_ref[0], where_ref[1]
    count = pair_ref.shape[2]
    mean, inverse = merged_stats(every_ref, count, 1e-05)
    factor = inverse * gain_ref[...]
    token = lax.broadcasted_iota(jnp.int32, (count, 640), 0)
    flat_ref[:, 5760:] = jnp.zeros((2 * count, 128), jnp.bfloat16)
    for row, (holder, which) in enumerate(((1, 1), (0, 0), (1, 0), (0, 1))):
        value = pair_ref[holder, which].astype(jnp.float32)
        value = (value - mean) * factor + shift_ref[...]
        value = value / (1.0 + jnp.exp(-value))
        if row == 0:
            value = jnp.where(chip > 0, value, 0.0)
        if row == 3:
            value = jnp.where(chip < PEERS // 2 - 1, value, 0.0)
        value = value.astype(jnp.bfloat16).astype(jnp.float32)
        shifts = (
            jnp.where(token == 0, 0.0, pltpu.roll(value, 1, 0)),
            value,
            jnp.where(token == count - 1, 0.0, pltpu.roll(value, count - 1, 0)),
        )
        for across, shifted in enumerate(shifts):
            shifted = shifted.astype(jnp.bfloat16)
            for out in range(2):
                down = row - out
                if 0 <= down <= 2:
                    at = (3 * down + across) * 640
                    flat_ref[out * count : (out + 1) * count, at : at + 640] = shifted
    for parity in range(2):

        @pl.when(core == parity)
        def _():
            for index in range(16):
                at = 360 * index + 180 * parity
                low = at // 128 * 128
                wide = flat_ref[:, low : low + 384]
                place = ROWS * (index % 4)
                out_ref[index // 4, :, place : place + ROWS] = wide[:, at - low : at - low + ROWS]


def time_embed(timestep, time_weight):
    half = TFREQ // 2
    index = jnp.arange(half, dtype=jnp.float32)
    freq = jnp.exp(-math.log(10000.0) * index / half)
    angle = timestep.astype(jnp.float32)[0] * freq
    feats = jnp.concatenate([jnp.cos(angle), jnp.sin(angle)])[None, :]
    return jnp.dot(feats, time_weight, precision=lax.Precision.HIGHEST)


def dot32(a, b):
    return jnp.dot(a, b, preferred_element_type=jnp.float32)


def dot_t(a, b):
    return lax.dot_general(
        a, b, (((1,), (1,)), ((), ())), preferred_element_type=jnp.float32
    )


def convolve(
    where_ref,
    blocks_ref,
    own_ref,
    left_ref,
    right_ref,
    low_ref,
    high_ref,
    kept_ref,
    given_ref,
    held_ref,
    sems,
):
    core, x = where_ref[0], where_ref[2]
    count = kept_ref.shape[0]
    copies, at = [], 0
    for index, ref in enumerate((own_ref, left_ref, right_ref, low_ref, high_ref)):
        size = ref.shape[0]
        copy = pltpu.make_async_copy(ref, held_ref.at[at : at + size], sems.at[index])
        copy.start()
        copies.append((copy, at))
        at += size
    total = None
    for step, parts in ((0, (0,)), (3, (1,)), (1, (2,)), (2, (3, 4))):
        for part in parts:
            copies[part][0].wait()
        at = copies[parts[0]][1]
        weight = held_ref[at : at + 4].reshape(4 * ROWS, -1)
        product = dot32(blocks_ref[(x + step) & 3], weight)
        total = product if total is None else total + product
    kept_ref[...] = jnp.where(core == 0, total[:count], total[count:])
    given_ref[...] = jnp.where(core == 0, total[count:], total[:count])


def middle(kept_ref, other_ref, latent_ref, bias_ref, mid_ref, stats_ref):
    conv = kept_ref[...] + other_ref[...]
    mid = (latent_ref[...].astype(jnp.float32) + conv + bias_ref[...]).astype(jnp.bfloat16)
    mid_ref[...] = mid
    stats = local_stats(mid.astype(jnp.float32))
    stats_ref[...] = jnp.broadcast_to(stats[None], stats_ref.shape)


def project(
    every_ref, mid_ref, other_ref, gain_ref, shift_ref, weight_ref, query_ref, fresh_ref, kept_ref
):
    count = mid_ref.shape[0]
    mean, inverse = merged_stats(every_ref, count, 1e-06)
    mid = jnp.concatenate([mid_ref[...], other_ref[...]], axis=0).astype(jnp.float32)
    normed = ((mid - mean) * (inverse * gain_ref[...]) + shift_ref[...]).astype(jnp.bfloat16)
    query = dot_t(normed, weight_ref[:384])
    lane = lax.broadcasted_iota(jnp.int32, query.shape, 1)
    query = jnp.where(lane < HEADS * HEAD_DIM, query, 0.0).astype(jnp.bfloat16)
    query_ref[...] = query * jnp.bfloat16(1.0 / math.sqrt(HEAD_DIM))
    fresh = dot_t(weight_ref[HEADS * HEAD_DIM :], normed[:count]).astype(jnp.bfloat16)
    fresh_ref[...] = fresh
    kept_ref[...] = fresh


def attention(q_ref, blocks, replaced, fresh_ref, before):
    count = q_ref.shape[0] // 2
    lane = lax.broadcasted_iota(jnp.int32, (2 * count, 128), 1)
    outs = []
    for head in range(HEADS):
        at = 128 * (head // 2)
        v_at = HEADS * HEAD_DIM + at
        mine = (lane < 64) if head % 2 == 0 else (lane >= 64)
        query = q_ref[:, at : at + 128].astype(jnp.float32)
        query = jnp.where(mine, query, 0.0).astype(jnp.bfloat16)
        last = head == HEADS - 1
        scores = []
        for index, parts in enumerate(blocks):
            keys = [ref[z, at : at + 128] for ref, z in parts]
            score = dot32(query, jnp.concatenate(keys, axis=1))
            if replaced is not None and index == 0:
                score = jnp.where(replaced, LOW, score)
            scores.append(score)
        values = []
        for parts in blocks:
            value = jnp.concatenate([ref[z, v_at : v_at + 128] for ref, z in parts], axis=1)
            values.append(value)
        if fresh_ref is not None:
            score = dot32(query[:count], fresh_ref[at : at + 128])
            score = jnp.concatenate([score, jnp.full((count, count), LOW, jnp.float32)], axis=0)
            scores.append(score)
            values.append(fresh_ref[v_at : v_at + 128])
        peak = scores[0].max(axis=1, keepdims=True)
        for score in scores[1:]:
            peak = jnp.maximum(peak, score.max(axis=1, keepdims=True))
        if before is None:
            total = jnp.zeros((2 * count, 1), jnp.float32)
            mixed = jnp.zeros((2 * count, 128), jnp.float32)
        else:
            held = before[:, 320 + head : 321 + head]
            peak = jnp.maximum(peak, held)
            factor = jnp.exp(held - peak)
            total = before[:, 328 + head : 329 + head] * factor
            mixed = before[:, at : at + 128] * factor
        for score, value in zip(scores, values, strict=True):
            weights = jnp.exp(score - peak)
            total = total + weights.sum(axis=1, keepdims=True)
            if last:
                value = jnp.concatenate([value, jnp.zeros_like(value)], axis=0)
            mixed = mixed + dot_t(weights.astype(jnp.bfloat16), value)
        outs.append((mixed, peak, total))
    stats = jnp.where(lane < 64, outs[4][0], 0.0)
    for head in range(HEADS):
        stats = jnp.where(lane == 64 + head, outs[head][1], stats)
        stats = jnp.where(lane == 72 + head, outs[head][2], stats)
    return (
        jnp.where(lane < 64, outs[0][0], outs[1][0]),
        jnp.where(lane < 64, outs[2][0], outs[3][0]),
        stats,
    )


def attend_near(where_ref, q_ref, own_ref, left_ref, fresh_ref, out_ref):
    my_z = where_ref[3]
    count = q_ref.shape[0] // 2
    row = lax.broadcasted_iota(jnp.int32, (2 * count, 4 * count), 0)
    block = lax.broadcasted_iota(jnp.int32, (2 * count, 4 * count), 1) // count
    replaced = (row < count) & (block == my_z)
    blocks = [[(ref, z) for z in range(4)] for ref in (own_ref, left_ref)]
    for tile, value in enumerate(attention(q_ref, blocks, replaced, fresh_ref, None)):
        out_ref[:, 128 * tile : 128 * (tile + 1)] = value


def attend_far(q_ref, right_ref, far_ref, near_ref, out_ref, given_ref):
    count = out_ref.shape[0]
    blocks = [[(ref, z) for z in range(4)] for ref in (right_ref, far_ref)]
    for tile, value in enumerate(attention(q_ref, blocks, None, None, near_ref)):
        out_ref[:, 128 * tile : 128 * (tile + 1)] = value[:count]
        given_ref[:, 128 * tile : 128 * (tile + 1)] = value[count:]


def finish(own_ref, other_ref, mid_ref, weight_ref, out_ref):
    count = mid_ref.shape[0]
    lane = lax.broadcasted_iota(jnp.int32, (count, 128), 1)
    factors = []
    for head in range(HEADS):
        peak1 = own_ref[:, 320 + head : 321 + head]
        peak2 = other_ref[:, 320 + head : 321 + head]
        peak = jnp.maximum(peak1, peak2)
        one, two = jnp.exp(peak1 - peak), jnp.exp(peak2 - peak)
        total = own_ref[:, 328 + head : 329 + head] * one
        total = total + other_ref[:, 328 + head : 329 + head] * two
        factors.append((one / total, two / total))
    result = mid_ref[...].astype(jnp.float32)
    for tile in range(3):
        first = factors[2 * tile]
        second = factors[min(2 * tile + 1, HEADS - 1)]
        at = 128 * tile
        mixed = own_ref[:, at : at + 128] * jnp.where(lane < 64, first[0], second[0])
        mixed = mixed + other_ref[:, at : at + 128] * jnp.where(lane < 64, first[1], second[1])
        mixed = mixed.astype(jnp.bfloat16)
        if tile == 2:
            mixed = mixed[:, :HEAD_DIM]
        result = result + dot32(mixed, weight_ref[at : at + mixed.shape[1]])
    out_ref[...] = result.astype(jnp.bfloat16)


def call(kernel, outs, smem, *args, scratch=(), fetched=(), cost=None):
    return pl.pallas_call(
        kernel,
        out_shape=[jax.ShapeDtypeStruct(shape, dtype) for shape, dtype in outs],
        in_specs=[
            SMEM if i < smem else pl.BlockSpec(memory_space=pl.ANY) if i in fetched else VMEM
            for i in range(len(args))
        ],
        out_specs=[VMEM] * len(outs),
        scratch_shapes=list(scratch),
        cost_estimate=cost,
        compiler_params=pltpu.CompilerParams(vmem_limit_bytes=40 * 1024 * 1024),
    )(*args)


def on_device(
    latent,
    timestep,
    norm1_gain,
    norm1_shift,
    conv_weight,
    conv_bias,
    time_weight,
    norm2_gain,
    norm2_shift,
    qkv_weight,
    out_weight,
    stale_kv,
):
    tok_dev, width = latent.shape
    feats = qkv_weight.shape[1] // 3
    me = lax.axis_index("space")
    where = jnp.stack([me % 2, me // 2, me // 8, (me // 2) % 4])
    rows = conv_weight.shape[0]
    f32, bf16 = jnp.float32, jnp.bfloat16
    table = ((PEERS, 8, 128), f32)

    weight = jnp.pad(conv_weight, ((0, ROWS - rows), (0, 0)))
    own_w = lax.all_gather(weight, "space", axis=0, axis_index_groups=Z_GROUPS)
    left_w = lax.ppermute(own_w, "space", RIGHT)
    right_w = lax.ppermute(own_w, "space", LEFT)
    outer = lax.ppermute(latent, "space", OUTER)
    (stats1,) = call(first_stats, [table], 0, latent)
    every1 = exchanged(stats1)
    pair = lax.all_gather(
        jnp.stack([latent, outer]), "space", axis=0, axis_index_groups=CORE_GROUPS
    )
    stale = stale_kv.transpose(0, 2, 1).reshape(2 * feats, tok_dev)
    stale, _ = lax.optimization_barrier((stale, own_w))
    own_kv = lax.all_gather(stale, "space", axis=0, axis_index_groups=Z_GROUPS)
    low_w = lax.ppermute(left_w[:2], "space", RIGHT)
    high_w = lax.ppermute(right_w[2:], "space", LEFT)
    (blocks,) = call(
        prepare,
        [((4, 2 * tok_dev, 4 * ROWS), bf16)],
        1,
        where,
        every1,
        pair,
        norm1_gain[None],
        norm1_shift[None],
        scratch=[pltpu.VMEM((2 * tok_dev, 5760 + 128), bf16)],
    )
    own_kv, _ = lax.optimization_barrier((own_kv, blocks))
    left_kv = lax.ppermute(own_kv, "space", RIGHT)
    right_kv = lax.ppermute(own_kv, "space", LEFT)
    step, _ = lax.optimization_barrier((timestep, blocks))
    bias = (conv_bias + time_embed(step, time_weight)).reshape(1, width)
    kept, given = call(
        convolve,
        [((tok_dev, width), f32)] * 2,
        1,
        where,
        blocks,
        own_w,
        left_w,
        right_w,
        low_w,
        high_w,
        scratch=[pltpu.VMEM((16, ROWS, width), bf16), pltpu.SemaphoreType.DMA((5,))],
        fetched=(2, 3, 4, 5, 6),
    )
    other = lax.ppermute(given, "space", SWAP)
    mid, stats2 = call(middle, [((tok_dev, width), bf16), table], 0, kept, other, latent, bias)
    every2 = exchanged(stats2)
    far_kv = lax.ppermute(left_kv, "space", RIGHT)
    query, fresh, kept_kv = call(
        project,
        [((2 * tok_dev, 384), bf16)] + [((2 * feats, tok_dev), bf16)] * 2,
        0,
        every2,
        mid,
        lax.ppermute(mid, "space", SWAP),
        norm2_gain[None],
        norm2_shift[None],
        qkv_weight.T,
    )
    fresh_kv = kept_kv.reshape(2, feats, tok_dev).transpose(0, 2, 1)
    (near,) = call(
        attend_near,
        [((2 * tok_dev, 384), f32)],
        1,
        where,
        query,
        own_kv,
        left_kv,
        fresh,
        cost=pl.CostEstimate(flops=2000000000, transcendentals=2 * 10**6, bytes_accessed=3 * 10**6),
    )
    mine, theirs = call(
        attend_far, [((tok_dev, 384), f32)] * 2, 0, query, right_kv, far_kv, near
    )
    other = lax.ppermute(theirs, "space", SWAP)
    (result,) = call(finish, [((tok_dev, width), bf16)], 0, mine, other, mid, out_weight)
    return (result, fresh_kv)


def solution(mesh):
    return jax.shard_map(
        on_device,
        mesh=mesh,
        in_specs=(
            P(("batch", "space"), None),
            P("batch"),
            P(),
            P(),
            P("space", None),
            P(),
            P(),
            P(),
            P(),
            P(),
            P(),
            P(None, ("batch", "space"), None),
        ),
        out_specs=(P(("batch", "space"), None), P(None, ("batch", "space"), None)),
        check_vma=False,
    )
```

```python
import math

import jax
import jax.numpy as jnp
from jax import lax
from jax.experimental import pallas as pl
from jax.experimental.pallas import tpu as pltpu
from jax.sharding import PartitionSpec as P

GROUPS = 32
HEADS = 5
HEAD_DIM = 64
TFREQ = 320
PER = 20
PEERS = 32
Z_GROUPS = [[8 * x + 2 * z + c for z in range(4)] for x in range(4) for c in range(2)]
CORE_GROUPS = [[2 * k, 2 * k + 1] for k in range(16)]
RIGHT = [(i, (i + 8) % PEERS) for i in range(PEERS)]
LEFT = [(i, (i + 24) % PEERS) for i in range(PEERS)]
SWAP = [(i, i ^ 1) for i in range(PEERS)]
OUTER = [(i, i - 2) for i in range(2, PEERS, 2)] + [(i, i + 2) for i in range(1, PEERS - 2, 2)]
ROWS = 192
LOW = -1e30
VMEM = pl.BlockSpec(memory_space=pltpu.VMEM)
SMEM = pl.BlockSpec(memory_space=pltpu.SMEM)


def group_map(first, transposed=False):
    shape = (128, 640) if transposed else (640, 128)
    channel = lax.broadcasted_iota(jnp.int32, shape, 1 if transposed else 0)
    low = (lax.broadcasted_iota(jnp.int32, shape, 0 if transposed else 1) - first) * PER
    return ((channel >= low) & (channel < low + PER)).astype(jnp.float32)


def exact(a, b):
    return jnp.dot(
        a, b, precision=lax.Precision.HIGHEST, preferred_element_type=jnp.float32
    )


def local_stats(values):
    count, width = values.shape
    summed = jnp.broadcast_to(values.sum(axis=0, keepdims=True), (8, width))
    mean = exact(summed, group_map(0)) / (count * PER)
    centered = values - exact(mean, group_map(0, True))[:1]
    spread = (centered * centered).sum(axis=0, keepdims=True)
    return mean + exact(jnp.broadcast_to(spread, (8, width)), group_map(GROUPS))


def merged_stats(every_ref, count, eps):
    every = every_ref[...]
    average = every.sum(axis=0) / PEERS
    shifted = every - average[None]
    between = (shifted * shifted).sum(axis=0) / PEERS
    var = pltpu.roll(average, 128 - GROUPS, 1) / (count * PER) + between
    lane = lax.broadcasted_iota(jnp.int32, var.shape, 1)
    inverse = jnp.where(lane < GROUPS, lax.rsqrt(var + eps), 0.0)
    spreading = group_map(0, True)
    return exact(average, spreading)[:1], exact(inverse, spreading)[:1]


def exchanged(stats):
    return lax.all_to_all(stats, "space", 0, 0, tiled=True)


def first_stats(latent_ref, out_ref):
    stats = local_stats(latent_ref[...].astype(jnp.float32))
    out_ref[...] = jnp.broadcast_to(stats[None], out_ref.shape)


def prepare(where_ref, every_ref, pair_ref, gain_ref, shift_ref, out_ref, flat_ref):
    core, chip = where_ref[0], where_ref[1]
    count = pair_ref.shape[2]
    mean, inverse = merged_stats(every_ref, count, 1e-05)
    factor = inverse * gain_ref[...]
    token = lax.broadcasted_iota(jnp.int32, (count, 640), 0)
    flat_ref[:, 5760:] = jnp.zeros((2 * count, 128), jnp.bfloat16)
    for row, (holder, which) in enumerate(((1, 1), (0, 0), (1, 0), (0, 1))):
        value = pair_ref[holder, which].astype(jnp.float32)
        value = (value - mean) * factor + shift_ref[...]
        value = value / (1.0 + jnp.exp(-value))
        if row == 0:
            value = jnp.where(chip > 0, value, 0.0)
        if row == 3:
            value = jnp.where(chip < PEERS // 2 - 1, value, 0.0)
        value = value.astype(jnp.bfloat16).astype(jnp.float32)
        shifts = (
            jnp.where(token == 0, 0.0, pltpu.roll(value, 1, 0)),
            value,
            jnp.where(token == count - 1, 0.0, pltpu.roll(value, count - 1, 0)),
        )
        for across, shifted in enumerate(shifts):
            shifted = shifted.astype(jnp.bfloat16)
            for out in range(2):
                down = row - out
                if 0 <= down <= 2:
                    at = (3 * down + across) * 640
                    flat_ref[out * count : (out + 1) * count, at : at + 640] = shifted
    for parity in range(2):

        @pl.when(core == parity)
        def _():
            for index in range(16):
                at = 360 * index + 180 * parity
                low = at // 128 * 128
                wide = flat_ref[:, low : low + 384]
                place = ROWS * (index % 4)
                out_ref[index // 4, :, place : place + ROWS] = wide[:, at - low : at - low + ROWS]


def time_embed(timestep, time_weight):
    half = TFREQ // 2
    index = jnp.arange(half, dtype=jnp.float32)
    freq = jnp.exp(-math.log(10000.0) * index / half)
    angle = timestep.astype(jnp.float32)[0] * freq
    feats = jnp.concatenate([jnp.cos(angle), jnp.sin(angle)])[None, :]
    return jnp.dot(feats, time_weight, precision=lax.Precision.HIGHEST)


def dot32(a, b):
    return jnp.dot(a, b, preferred_element_type=jnp.float32)


def dot_t(a, b):
    return lax.dot_general(
        a, b, (((1,), (1,)), ((), ())), preferred_element_type=jnp.float32
    )


def convolve(
    where_ref,
    blocks_ref,
    own_ref,
    left_ref,
    right_ref,
    low_ref,
    high_ref,
    kept_ref,
    given_ref,
    held_ref,
    sems,
):
    core, x = where_ref[0], where_ref[2]
    count = kept_ref.shape[0]
    copies, at = [], 0
    for index, ref in enumerate((own_ref, left_ref, right_ref, low_ref, high_ref)):
        size = ref.shape[0]
        copy = pltpu.make_async_copy(ref, held_ref.at[at : at + size], sems.at[index])
        copy.start()
        copies.append((copy, at))
        at += size
    total = None
    for step, parts in ((0, (0,)), (3, (1,)), (1, (2,)), (2, (3, 4))):
        for part in parts:
            copies[part][0].wait()
        at = copies[parts[0]][1]
        weight = held_ref[at : at + 4].reshape(4 * ROWS, -1)
        product = dot32(blocks_ref[(x + step) & 3], weight)
        total = product if total is None else total + product
    kept_ref[...] = jnp.where(core == 0, total[:count], total[count:])
    given_ref[...] = jnp.where(core == 0, total[count:], total[:count])


def middle(kept_ref, other_ref, latent_ref, bias_ref, mid_ref, stats_ref):
    conv = kept_ref[...] + other_ref[...]
    mid = (latent_ref[...].astype(jnp.float32) + conv + bias_ref[...]).astype(jnp.bfloat16)
    mid_ref[...] = mid
    stats = local_stats(mid.astype(jnp.float32))
    stats_ref[...] = jnp.broadcast_to(stats[None], stats_ref.shape)


def project(
    every_ref, mid_ref, other_ref, gain_ref, shift_ref, weight_ref, query_ref, fresh_ref, kept_ref
):
    count = mid_ref.shape[0]
    mean, inverse = merged_stats(every_ref, count, 1e-06)
    mid = jnp.concatenate([mid_ref[...], other_ref[...]], axis=0).astype(jnp.float32)
    normed = ((mid - mean) * (inverse * gain_ref[...]) + shift_ref[...]).astype(jnp.bfloat16)
    query = dot_t(normed, weight_ref[:384])
    lane = lax.broadcasted_iota(jnp.int32, query.shape, 1)
    query = jnp.where(lane < HEADS * HEAD_DIM, query, 0.0).astype(jnp.bfloat16)
    query_ref[...] = query * jnp.bfloat16(1.0 / math.sqrt(HEAD_DIM))
    fresh = dot_t(weight_ref[HEADS * HEAD_DIM :], normed[:count]).astype(jnp.bfloat16)
    fresh_ref[...] = fresh
    kept_ref[...] = fresh


def attention(q_ref, blocks, replaced, fresh_ref, before):
    count = q_ref.shape[0] // 2
    lane = lax.broadcasted_iota(jnp.int32, (2 * count, 128), 1)
    outs = []
    for head in range(HEADS):
        at = 128 * (head // 2)
        v_at = HEADS * HEAD_DIM + at
        mine = (lane < 64) if head % 2 == 0 else (lane >= 64)
        query = q_ref[:, at : at + 128].astype(jnp.float32)
        query = jnp.where(mine, query, 0.0).astype(jnp.bfloat16)
        last = head == HEADS - 1
        scores = []
        for index, parts in enumerate(blocks):
            keys = [ref[z, at : at + 128] for ref, z in parts]
            score = dot32(query, jnp.concatenate(keys, axis=1))
            if replaced is not None and index == 0:
                score = jnp.where(replaced, LOW, score)
            scores.append(score)
        values = []
        for parts in blocks:
            value = jnp.concatenate([ref[z, v_at : v_at + 128] for ref, z in parts], axis=1)
            values.append(value)
        if fresh_ref is not None:
            score = dot32(query[:count], fresh_ref[at : at + 128])
            score = jnp.concatenate([score, jnp.full((count, count), LOW, jnp.float32)], axis=0)
            scores.append(score)
            values.append(fresh_ref[v_at : v_at + 128])
        peak = scores[0].max(axis=1, keepdims=True)
        for score in scores[1:]:
            peak = jnp.maximum(peak, score.max(axis=1, keepdims=True))
        if before is None:
            total = jnp.zeros((2 * count, 1), jnp.float32)
            mixed = jnp.zeros((2 * count, 128), jnp.float32)
        else:
            held = before[:, 320 + head : 321 + head]
            peak = jnp.maximum(peak, held)
            factor = jnp.exp(held - peak)
            total = before[:, 328 + head : 329 + head] * factor
            mixed = before[:, at : at + 128] * factor
        for score, value in zip(scores, values, strict=True):
            weights = jnp.exp(score - peak)
            total = total + weights.sum(axis=1, keepdims=True)
            if last:
                value = jnp.concatenate([value, jnp.zeros_like(value)], axis=0)
            mixed = mixed + dot_t(weights.astype(jnp.bfloat16), value)
        outs.append((mixed, peak, total))
    stats = jnp.where(lane < 64, outs[4][0], 0.0)
    for head in range(HEADS):
        stats = jnp.where(lane == 64 + head, outs[head][1], stats)
        stats = jnp.where(lane == 72 + head, outs[head][2], stats)
    return (
        jnp.where(lane < 64, outs[0][0], outs[1][0]),
        jnp.where(lane < 64, outs[2][0], outs[3][0]),
        stats,
    )


def attend_near(where_ref, q_ref, own_ref, left_ref, right_ref, fresh_ref, out_ref):
    my_z = where_ref[3]
    count = q_ref.shape[0] // 2
    row = lax.broadcasted_iota(jnp.int32, (2 * count, 4 * count), 0)
    block = lax.broadcasted_iota(jnp.int32, (2 * count, 4 * count), 1) // count
    replaced = (row < count) & (block == my_z)
    blocks = [[(ref, z) for z in range(4)] for ref in (own_ref, left_ref, right_ref)]
    for tile, value in enumerate(attention(q_ref, blocks, replaced, fresh_ref, None)):
        out_ref[:, 128 * tile : 128 * (tile + 1)] = value


def attend_far(q_ref, far_ref, near_ref, out_ref, given_ref):
    count = out_ref.shape[0]
    blocks = [[(far_ref, z) for z in range(4)]]
    for tile, value in enumerate(attention(q_ref, blocks, None, None, near_ref)):
        out_ref[:, 128 * tile : 128 * (tile + 1)] = value[:count]
        given_ref[:, 128 * tile : 128 * (tile + 1)] = value[count:]


def finish(own_ref, other_ref, mid_ref, weight_ref, out_ref):
    count = mid_ref.shape[0]
    lane = lax.broadcasted_iota(jnp.int32, (count, 128), 1)
    factors = []
    for head in range(HEADS):
        peak1 = own_ref[:, 320 + head : 321 + head]
        peak2 = other_ref[:, 320 + head : 321 + head]
        peak = jnp.maximum(peak1, peak2)
        one, two = jnp.exp(peak1 - peak), jnp.exp(peak2 - peak)
        total = own_ref[:, 328 + head : 329 + head] * one
        total = total + other_ref[:, 328 + head : 329 + head] * two
        factors.append((one / total, two / total))
    result = mid_ref[...].astype(jnp.float32)
    for tile in range(3):
        first = factors[2 * tile]
        second = factors[min(2 * tile + 1, HEADS - 1)]
        at = 128 * tile
        mixed = own_ref[:, at : at + 128] * jnp.where(lane < 64, first[0], second[0])
        mixed = mixed + other_ref[:, at : at + 128] * jnp.where(lane < 64, first[1], second[1])
        mixed = mixed.astype(jnp.bfloat16)
        if tile == 2:
            mixed = mixed[:, :HEAD_DIM]
        result = result + dot32(mixed, weight_ref[at : at + mixed.shape[1]])
    out_ref[...] = result.astype(jnp.bfloat16)


def call(kernel, outs, smem, *args, scratch=(), fetched=(), cost=None):
    return pl.pallas_call(
        kernel,
        out_shape=[jax.ShapeDtypeStruct(shape, dtype) for shape, dtype in outs],
        in_specs=[
            SMEM if i < smem else pl.BlockSpec(memory_space=pl.ANY) if i in fetched else VMEM
            for i in range(len(args))
        ],
        out_specs=[VMEM] * len(outs),
        scratch_shapes=list(scratch),
        cost_estimate=cost,
        compiler_params=pltpu.CompilerParams(vmem_limit_bytes=40 * 1024 * 1024),
    )(*args)


def on_device(
    latent,
    timestep,
    norm1_gain,
    norm1_shift,
    conv_weight,
    conv_bias,
    time_weight,
    norm2_gain,
    norm2_shift,
    qkv_weight,
    out_weight,
    stale_kv,
):
    tok_dev, width = latent.shape
    feats = qkv_weight.shape[1] // 3
    me = lax.axis_index("space")
    where = jnp.stack([me % 2, me // 2, me // 8, (me // 2) % 4])
    rows = conv_weight.shape[0]
    f32, bf16 = jnp.float32, jnp.bfloat16
    table = ((PEERS, 8, 128), f32)

    weight = jnp.pad(conv_weight, ((0, ROWS - rows), (0, 0)))
    own_w = lax.all_gather(weight, "space", axis=0, axis_index_groups=Z_GROUPS)
    left_w = lax.ppermute(own_w, "space", RIGHT)
    right_w = lax.ppermute(own_w, "space", LEFT)
    outer = lax.ppermute(latent, "space", OUTER)
    (stats1,) = call(first_stats, [table], 0, latent)
    every1 = exchanged(stats1)
    pair = lax.all_gather(
        jnp.stack([latent, outer]), "space", axis=0, axis_index_groups=CORE_GROUPS
    )
    stale = stale_kv.transpose(0, 2, 1).reshape(2 * feats, tok_dev)
    stale, _ = lax.optimization_barrier((stale, own_w))
    own_kv = lax.all_gather(stale, "space", axis=0, axis_index_groups=Z_GROUPS)
    low_w = lax.ppermute(left_w[:2], "space", RIGHT)
    high_w = lax.ppermute(right_w[2:], "space", LEFT)
    (blocks,) = call(
        prepare,
        [((4, 2 * tok_dev, 4 * ROWS), bf16)],
        1,
        where,
        every1,
        pair,
        norm1_gain[None],
        norm1_shift[None],
        scratch=[pltpu.VMEM((2 * tok_dev, 5760 + 128), bf16)],
    )
    own_kv, _ = lax.optimization_barrier((own_kv, pair))
    left_kv = lax.ppermute(own_kv, "space", RIGHT)
    right_kv = lax.ppermute(own_kv, "space", LEFT)
    step, _ = lax.optimization_barrier((timestep, blocks))
    bias = (conv_bias + time_embed(step, time_weight)).reshape(1, width)
    kept, given = call(
        convolve,
        [((tok_dev, width), f32)] * 2,
        1,
        where,
        blocks,
        own_w,
        left_w,
        right_w,
        low_w,
        high_w,
        scratch=[pltpu.VMEM((16, ROWS, width), bf16), pltpu.SemaphoreType.DMA((5,))],
        fetched=(2, 3, 4, 5, 6),
    )
    other = lax.ppermute(given, "space", SWAP)
    mid, stats2 = call(middle, [((tok_dev, width), bf16), table], 0, kept, other, latent, bias)
    every2 = exchanged(stats2)
    far_kv = lax.ppermute(left_kv, "space", RIGHT)
    query, fresh, kept_kv = call(
        project,
        [((2 * tok_dev, 384), bf16)] + [((2 * feats, tok_dev), bf16)] * 2,
        0,
        every2,
        mid,
        lax.ppermute(mid, "space", SWAP),
        norm2_gain[None],
        norm2_shift[None],
        qkv_weight.T,
    )
    fresh_kv = kept_kv.reshape(2, feats, tok_dev).transpose(0, 2, 1)
    (near,) = call(
        attend_near,
        [((2 * tok_dev, 384), f32)],
        1,
        where,
        query,
        own_kv,
        left_kv,
        right_kv,
        fresh,
        cost=pl.CostEstimate(flops=2000000000, transcendentals=2 * 10**6, bytes_accessed=3 * 10**6),
    )
    mine, theirs = call(
        attend_far, [((tok_dev, 384), f32)] * 2, 0, query, far_kv, near
    )
    other = lax.ppermute(theirs, "space", SWAP)
    (result,) = call(finish, [((tok_dev, width), bf16)], 0, mine, other, mid, out_weight)
    return (result, fresh_kv)


def solution(mesh):
    return jax.shard_map(
        on_device,
        mesh=mesh,
        in_specs=(
            P(("batch", "space"), None),
            P("batch"),
            P(),
            P(),
            P("space", None),
            P(),
            P(),
            P(),
            P(),
            P(),
            P(),
            P(None, ("batch", "space"), None),
        ),
        out_specs=(P(("batch", "space"), None), P(None, ("batch", "space"), None)),
        check_vma=False,
    )
```

```python
import math

import jax
import jax.numpy as jnp
from jax import lax
from jax.experimental import pallas as pl
from jax.experimental.pallas import tpu as pltpu
from jax.sharding import PartitionSpec as P

GROUPS = 32
HEADS = 5
HEAD_DIM = 64
TFREQ = 320
PER = 20
PEERS = 32
Z_GROUPS = [[8 * x + 2 * z + c for z in range(4)] for x in range(4) for c in range(2)]
CORE_GROUPS = [[2 * k, 2 * k + 1] for k in range(16)]
RIGHT = [(i, (i + 8) % PEERS) for i in range(PEERS)]
LEFT = [(i, (i + 24) % PEERS) for i in range(PEERS)]
SWAP = [(i, i ^ 1) for i in range(PEERS)]
OUTER = [(i, i - 2) for i in range(2, PEERS, 2)] + [(i, i + 2) for i in range(1, PEERS - 2, 2)]
ROWS = 192
LOW = -1e30
VMEM = pl.BlockSpec(memory_space=pltpu.VMEM)
SMEM = pl.BlockSpec(memory_space=pltpu.SMEM)


def group_map(first, transposed=False):
    shape = (128, 640) if transposed else (640, 128)
    channel = lax.broadcasted_iota(jnp.int32, shape, 1 if transposed else 0)
    low = (lax.broadcasted_iota(jnp.int32, shape, 0 if transposed else 1) - first) * PER
    return ((channel >= low) & (channel < low + PER)).astype(jnp.float32)


def exact(a, b):
    return jnp.dot(
        a, b, precision=lax.Precision.HIGHEST, preferred_element_type=jnp.float32
    )


def local_stats(values):
    count, width = values.shape
    summed = jnp.broadcast_to(values.sum(axis=0, keepdims=True), (8, width))
    mean = exact(summed, group_map(0)) / (count * PER)
    centered = values - exact(mean, group_map(0, True))[:1]
    spread = (centered * centered).sum(axis=0, keepdims=True)
    return mean + exact(jnp.broadcast_to(spread, (8, width)), group_map(GROUPS))


def merged_stats(every_ref, count, eps):
    every = every_ref[...]
    average = every.sum(axis=0) / PEERS
    shifted = every - average[None]
    between = (shifted * shifted).sum(axis=0) / PEERS
    var = pltpu.roll(average, 128 - GROUPS, 1) / (count * PER) + between
    lane = lax.broadcasted_iota(jnp.int32, var.shape, 1)
    inverse = jnp.where(lane < GROUPS, lax.rsqrt(var + eps), 0.0)
    spreading = group_map(0, True)
    return exact(average, spreading)[:1], exact(inverse, spreading)[:1]


def exchanged(stats):
    return lax.all_to_all(stats, "space", 0, 0, tiled=True)


def first_stats(latent_ref, out_ref):
    stats = local_stats(latent_ref[...].astype(jnp.float32))
    out_ref[...] = jnp.broadcast_to(stats[None], out_ref.shape)


def prepare(where_ref, every_ref, pair_ref, gain_ref, shift_ref, out_ref, flat_ref):
    core, chip = where_ref[0], where_ref[1]
    count = pair_ref.shape[2]
    mean, inverse = merged_stats(every_ref, count, 1e-05)
    factor = inverse * gain_ref[...]
    token = lax.broadcasted_iota(jnp.int32, (count, 640), 0)
    flat_ref[:, 5760:] = jnp.zeros((2 * count, 128), jnp.bfloat16)
    for row, (holder, which) in enumerate(((1, 1), (0, 0), (1, 0), (0, 1))):
        value = pair_ref[holder, which].astype(jnp.float32)
        value = (value - mean) * factor + shift_ref[...]
        value = value / (1.0 + jnp.exp(-value))
        if row == 0:
            value = jnp.where(chip > 0, value, 0.0)
        if row == 3:
            value = jnp.where(chip < PEERS // 2 - 1, value, 0.0)
        value = value.astype(jnp.bfloat16).astype(jnp.float32)
        shifts = (
            jnp.where(token == 0, 0.0, pltpu.roll(value, 1, 0)),
            value,
            jnp.where(token == count - 1, 0.0, pltpu.roll(value, count - 1, 0)),
        )
        for across, shifted in enumerate(shifts):
            shifted = shifted.astype(jnp.bfloat16)
            for out in range(2):
                down = row - out
                if 0 <= down <= 2:
                    at = (3 * down + across) * 640
                    flat_ref[out * count : (out + 1) * count, at : at + 640] = shifted
    for parity in range(2):

        @pl.when(core == parity)
        def _():
            for index in range(16):
                at = 360 * index + 180 * parity
                low = at // 128 * 128
                wide = flat_ref[:, low : low + 384]
                place = ROWS * (index % 4)
                out_ref[index // 4, :, place : place + ROWS] = wide[:, at - low : at - low + ROWS]


def time_embed(timestep, time_weight):
    half = TFREQ // 2
    index = jnp.arange(half, dtype=jnp.float32)
    freq = jnp.exp(-math.log(10000.0) * index / half)
    angle = timestep.astype(jnp.float32)[0] * freq
    feats = jnp.concatenate([jnp.cos(angle), jnp.sin(angle)])[None, :]
    return jnp.dot(feats, time_weight, precision=lax.Precision.HIGHEST)


def dot32(a, b):
    return jnp.dot(a, b, preferred_element_type=jnp.float32)


def dot_t(a, b):
    return lax.dot_general(
        a, b, (((1,), (1,)), ((), ())), preferred_element_type=jnp.float32
    )


def convolve(
    where_ref,
    blocks_ref,
    own_ref,
    left_ref,
    right_ref,
    low_ref,
    high_ref,
    kept_ref,
    given_ref,
    held_ref,
    sems,
):
    core, x = where_ref[0], where_ref[2]
    count = kept_ref.shape[0]
    copies, at = [], 0
    for index, ref in enumerate((own_ref, left_ref, right_ref, low_ref, high_ref)):
        size = ref.shape[0]
        copy = pltpu.make_async_copy(ref, held_ref.at[at : at + size], sems.at[index])
        copy.start()
        copies.append((copy, at))
        at += size
    total = None
    for step, parts in ((0, (0,)), (3, (1,)), (1, (2,)), (2, (3, 4))):
        for part in parts:
            copies[part][0].wait()
        at = copies[parts[0]][1]
        weight = held_ref[at : at + 4].reshape(4 * ROWS, -1)
        product = dot32(blocks_ref[(x + step) & 3], weight)
        total = product if total is None else total + product
    kept_ref[...] = jnp.where(core == 0, total[:count], total[count:])
    given_ref[...] = jnp.where(core == 0, total[count:], total[:count])


def middle(kept_ref, other_ref, latent_ref, bias_ref, mid_ref, stats_ref):
    conv = kept_ref[...] + other_ref[...]
    mid = (latent_ref[...].astype(jnp.float32) + conv + bias_ref[...]).astype(jnp.bfloat16)
    mid_ref[...] = mid
    stats = local_stats(mid.astype(jnp.float32))
    stats_ref[...] = jnp.broadcast_to(stats[None], stats_ref.shape)


def project(
    every_ref, mid_ref, other_ref, gain_ref, shift_ref, weight_ref, query_ref, fresh_ref, kept_ref
):
    count = mid_ref.shape[0]
    mean, inverse = merged_stats(every_ref, count, 1e-06)
    mid = jnp.concatenate([mid_ref[...], other_ref[...]], axis=0).astype(jnp.float32)
    normed = ((mid - mean) * (inverse * gain_ref[...]) + shift_ref[...]).astype(jnp.bfloat16)
    query = dot_t(normed, weight_ref[:384])
    lane = lax.broadcasted_iota(jnp.int32, query.shape, 1)
    query = jnp.where(lane < HEADS * HEAD_DIM, query, 0.0).astype(jnp.bfloat16)
    query_ref[...] = query * jnp.bfloat16(1.0 / math.sqrt(HEAD_DIM))
    fresh = dot_t(weight_ref[HEADS * HEAD_DIM :], normed[:count]).astype(jnp.bfloat16)
    fresh_ref[...] = fresh
    kept_ref[...] = fresh


def attention(q_ref, blocks, replaced, fresh_ref, before):
    count = q_ref.shape[0] // 2
    lane = lax.broadcasted_iota(jnp.int32, (2 * count, 128), 1)
    outs = []
    for head in range(HEADS):
        at = 128 * (head // 2)
        v_at = HEADS * HEAD_DIM + at
        mine = (lane < 64) if head % 2 == 0 else (lane >= 64)
        query = q_ref[:, at : at + 128].astype(jnp.float32)
        query = jnp.where(mine, query, 0.0).astype(jnp.bfloat16)
        last = head == HEADS - 1
        scores = []
        for index, parts in enumerate(blocks):
            keys = [ref[z, at : at + 128] for ref, z in parts]
            score = dot32(query, jnp.concatenate(keys, axis=1))
            if replaced is not None and index == 0:
                score = jnp.where(replaced, LOW, score)
            scores.append(score)
        values = []
        for parts in blocks:
            value = jnp.concatenate([ref[z, v_at : v_at + 128] for ref, z in parts], axis=1)
            values.append(value)
        if fresh_ref is not None:
            score = dot32(query[:count], fresh_ref[at : at + 128])
            score = jnp.concatenate([score, jnp.full((count, count), LOW, jnp.float32)], axis=0)
            scores.append(score)
            values.append(fresh_ref[v_at : v_at + 128])
        peak = scores[0].max(axis=1, keepdims=True)
        for score in scores[1:]:
            peak = jnp.maximum(peak, score.max(axis=1, keepdims=True))
        if before is None:
            total = jnp.zeros((2 * count, 1), jnp.float32)
            mixed = jnp.zeros((2 * count, 128), jnp.float32)
        else:
            held = before[:, 320 + head : 321 + head]
            peak = jnp.maximum(peak, held)
            factor = jnp.exp(held - peak)
            total = before[:, 328 + head : 329 + head] * factor
            mixed = before[:, at : at + 128] * factor
        for score, value in zip(scores, values, strict=True):
            weights = jnp.exp(score - peak)
            total = total + weights.sum(axis=1, keepdims=True)
            if last:
                value = jnp.concatenate([value, jnp.zeros_like(value)], axis=0)
            mixed = mixed + dot_t(weights.astype(jnp.bfloat16), value)
        outs.append((mixed, peak, total))
    stats = jnp.where(lane < 64, outs[4][0], 0.0)
    for head in range(HEADS):
        stats = jnp.where(lane == 64 + head, outs[head][1], stats)
        stats = jnp.where(lane == 72 + head, outs[head][2], stats)
    return (
        jnp.where(lane < 64, outs[0][0], outs[1][0]),
        jnp.where(lane < 64, outs[2][0], outs[3][0]),
        stats,
    )


def attend_near(where_ref, q_ref, own_ref, left_ref, right_ref, fresh_ref, out_ref):
    my_z = where_ref[3]
    count = q_ref.shape[0] // 2
    row = lax.broadcasted_iota(jnp.int32, (2 * count, 4 * count), 0)
    block = lax.broadcasted_iota(jnp.int32, (2 * count, 4 * count), 1) // count
    replaced = (row < count) & (block == my_z)
    blocks = [[(ref, z) for z in range(4)] for ref in (own_ref, left_ref, right_ref)]
    for tile, value in enumerate(attention(q_ref, blocks, replaced, fresh_ref, None)):
        out_ref[:, 128 * tile : 128 * (tile + 1)] = value


def attend_far(q_ref, low_ref, high_ref, near_ref, out_ref, given_ref):
    count = out_ref.shape[0]
    blocks = [[(low_ref, 0), (low_ref, 1), (high_ref, 0), (high_ref, 1)]]
    for tile, value in enumerate(attention(q_ref, blocks, None, None, near_ref)):
        out_ref[:, 128 * tile : 128 * (tile + 1)] = value[:count]
        given_ref[:, 128 * tile : 128 * (tile + 1)] = value[count:]


def finish(own_ref, other_ref, mid_ref, weight_ref, out_ref):
    count = mid_ref.shape[0]
    lane = lax.broadcasted_iota(jnp.int32, (count, 128), 1)
    factors = []
    for head in range(HEADS):
        peak1 = own_ref[:, 320 + head : 321 + head]
        peak2 = other_ref[:, 320 + head : 321 + head]
        peak = jnp.maximum(peak1, peak2)
        one, two = jnp.exp(peak1 - peak), jnp.exp(peak2 - peak)
        total = own_ref[:, 328 + head : 329 + head] * one
        total = total + other_ref[:, 328 + head : 329 + head] * two
        factors.append((one / total, two / total))
    result = mid_ref[...].astype(jnp.float32)
    for tile in range(3):
        first = factors[2 * tile]
        second = factors[min(2 * tile + 1, HEADS - 1)]
        at = 128 * tile
        mixed = own_ref[:, at : at + 128] * jnp.where(lane < 64, first[0], second[0])
        mixed = mixed + other_ref[:, at : at + 128] * jnp.where(lane < 64, first[1], second[1])
        mixed = mixed.astype(jnp.bfloat16)
        if tile == 2:
            mixed = mixed[:, :HEAD_DIM]
        result = result + dot32(mixed, weight_ref[at : at + mixed.shape[1]])
    out_ref[...] = result.astype(jnp.bfloat16)


def call(kernel, outs, smem, *args, scratch=(), fetched=(), cost=None):
    return pl.pallas_call(
        kernel,
        out_shape=[jax.ShapeDtypeStruct(shape, dtype) for shape, dtype in outs],
        in_specs=[
            SMEM if i < smem else pl.BlockSpec(memory_space=pl.ANY) if i in fetched else VMEM
            for i in range(len(args))
        ],
        out_specs=[VMEM] * len(outs),
        scratch_shapes=list(scratch),
        cost_estimate=cost,
        compiler_params=pltpu.CompilerParams(vmem_limit_bytes=40 * 1024 * 1024),
    )(*args)


def on_device(
    latent,
    timestep,
    norm1_gain,
    norm1_shift,
    conv_weight,
    conv_bias,
    time_weight,
    norm2_gain,
    norm2_shift,
    qkv_weight,
    out_weight,
    stale_kv,
):
    tok_dev, width = latent.shape
    feats = qkv_weight.shape[1] // 3
    me = lax.axis_index("space")
    where = jnp.stack([me % 2, me // 2, me // 8, (me // 2) % 4])
    rows = conv_weight.shape[0]
    f32, bf16 = jnp.float32, jnp.bfloat16
    table = ((PEERS, 8, 128), f32)

    weight = jnp.pad(conv_weight, ((0, ROWS - rows), (0, 0)))
    own_w = lax.all_gather(weight, "space", axis=0, axis_index_groups=Z_GROUPS)
    left_w = lax.ppermute(own_w, "space", RIGHT)
    right_w = lax.ppermute(own_w, "space", LEFT)
    outer = lax.ppermute(latent, "space", OUTER)
    (stats1,) = call(first_stats, [table], 0, latent)
    every1 = exchanged(stats1)
    pair = lax.all_gather(
        jnp.stack([latent, outer]), "space", axis=0, axis_index_groups=CORE_GROUPS
    )
    stale = stale_kv.transpose(0, 2, 1).reshape(2 * feats, tok_dev)
    stale, _ = lax.optimization_barrier((stale, own_w))
    own_kv = lax.all_gather(stale, "space", axis=0, axis_index_groups=Z_GROUPS)
    left_w, right_w, own_kv = lax.optimization_barrier((left_w, right_w, own_kv))
    low_w = lax.ppermute(left_w[:2], "space", RIGHT)
    high_w = lax.ppermute(right_w[2:], "space", LEFT)
    (blocks,) = call(
        prepare,
        [((4, 2 * tok_dev, 4 * ROWS), bf16)],
        1,
        where,
        every1,
        pair,
        norm1_gain[None],
        norm1_shift[None],
        scratch=[pltpu.VMEM((2 * tok_dev, 5760 + 128), bf16)],
    )
    own_kv, _ = lax.optimization_barrier((own_kv, pair))
    left_kv = lax.ppermute(own_kv, "space", RIGHT)
    right_kv = lax.ppermute(own_kv, "space", LEFT)
    step, _ = lax.optimization_barrier((timestep, blocks))
    bias = (conv_bias + time_embed(step, time_weight)).reshape(1, width)
    kept, given = call(
        convolve,
        [((tok_dev, width), f32)] * 2,
        1,
        where,
        blocks,
        own_w,
        left_w,
        right_w,
        low_w,
        high_w,
        scratch=[pltpu.VMEM((16, ROWS, width), bf16), pltpu.SemaphoreType.DMA((5,))],
        fetched=(2, 3, 4, 5, 6),
    )
    other = lax.ppermute(given, "space", SWAP)
    mid, stats2 = call(middle, [((tok_dev, width), bf16), table], 0, kept, other, latent, bias)
    every2 = exchanged(stats2)
    low_kv = lax.ppermute(left_kv[:2], "space", RIGHT)
    high_kv = lax.ppermute(right_kv[2:], "space", LEFT)
    query, fresh, kept_kv = call(
        project,
        [((2 * tok_dev, 384), bf16)] + [((2 * feats, tok_dev), bf16)] * 2,
        0,
        every2,
        mid,
        lax.ppermute(mid, "space", SWAP),
        norm2_gain[None],
        norm2_shift[None],
        qkv_weight.T,
    )
    fresh_kv = kept_kv.reshape(2, feats, tok_dev).transpose(0, 2, 1)
    (near,) = call(
        attend_near,
        [((2 * tok_dev, 384), f32)],
        1,
        where,
        query,
        own_kv,
        left_kv,
        right_kv,
        fresh,
        cost=pl.CostEstimate(flops=1000000000, transcendentals=2 * 10**6, bytes_accessed=3 * 10**6),
    )
    mine, theirs = call(
        attend_far, [((tok_dev, 384), f32)] * 2, 0, query, low_kv, high_kv, near
    )
    other = lax.ppermute(theirs, "space", SWAP)
    (result,) = call(finish, [((tok_dev, width), bf16)], 0, mine, other, mid, out_weight)
    return (result, fresh_kv)


def solution(mesh):
    return jax.shard_map(
        on_device,
        mesh=mesh,
        in_specs=(
            P(("batch", "space"), None),
            P("batch"),
            P(),
            P(),
            P("space", None),
            P(),
            P(),
            P(),
            P(),
            P(),
            P(),
            P(None, ("batch", "space"), None),
        ),
        out_specs=(P(("batch", "space"), None), P(None, ("batch", "space"), None)),
        check_vma=False,
    )
```
